128 devices in a mesh: tm: 8 (over z_hi, y), space: 16 (over x, z_lo, core).
Axes of the slice: x: 4, y: 4, z: 4 (z_hi: 2, z_lo: 2; z = z_hi * 2 + z_lo), core: 2. Of those that a mesh axis runs over, the one named last changes fastest.
Arguments:
- dual_model: float32 [8, 32, 1024, 512], P('tm', None, 'space'), may hold values from -6 to 6
- state_incr: float32 [8, 32, 1024, 512], P('tm', None, 'space'), may hold values from -6 to 6
- dual_obs: float32 [8, 384, 32, 128], P('tm', 'space'), may hold values from -6 to 6
- model_var: float32 [8, 32, 1024, 512], P('tm', None, 'space'), may hold values from 0.2 to 2
- obs_var: float32 [8, 384, 32, 128], P('tm', 'space'), may hold values from 0.2 to 2
- level_mix: float32 [8, 32, 32], P('tm'), may hold values from -1 to 1, as said below
- diffusivity: float32 [8, 1024, 512], P('tm', 'space'), may hold values from 0.02 to 0.22
- obs_tile: int32 [8, 384, 1], P('tm', 'space'), may hold values from 0 to 15; in each aligned block of 24 rows (0 to 23, 24 to 47, ..., all dimensions but the last counted through in order) at most 4 rows name the same one
- obs_cells: int32 [8, 16, 16, 4, 4, 128], P('tm', 'space'), may hold values from 0 to 32767
- obs_weights: float32 [8, 16, 16, 4, 4, 128], P('tm', 'space'), may hold values from 0.1 to 0.5
Outputs:
- model_rows: float32 [8, 32, 1024, 512], P('tm', None, 'space')
- obs_rows: float32 [8, 384, 32, 128], P('tm', 'space')
- state_rows: float32 [8, 32, 1024, 512], P('tm', None, 'space')
The draws below stay inside these ranges and needn't reach their ends.
Inputs may be any that keep to these rules, and one draw needn't show every extreme that they name: `obs_tile`: among the 24 blocks of one owner in one subwindow no tile is named more than 4 times, a bound that some block reaches. `level_mix`: each matrix has a diagonal of 0.5 to 0.9 and independent off-diagonal entries.
All inputs are finite; a program needn't handle non-finite values.
Results may differ from the reference program's by a relative error of at most 0.0003.
Values sent between devices are 32-bit elements; how exact they have to be, the bound alone decides.
No kernel may reach another device: no remote copies, remote signals or barrier semaphores. Data moves between devices by JAX's collectives and lax.ppermute only.
A program may use at most 192 MiB of HBM per device.

```python
import math
import jax
import jax.numpy as jnp
import numpy as np
from jax import lax

LEV = 32
OB = 128
TAPS = 4
MOST = 4
CX = 64
NY = 512
NB_DEV = 24
SUBS = 8
NX = 1024
NBLOCKS = 384
N_SPACE = 16


def draw_level_mix(key, part):
    key = jax.random.fold_in(key, 7)
    first, second = jax.random.split(key)
    diag = jax.random.uniform(first, (SUBS, LEV), jnp.float32, 0.5, 0.9)
    offdiag = jnp.clip(jax.random.normal(second, (SUBS, LEV, LEV), jnp.float32), -3.0, 3.0) * (0.3 / math.sqrt(LEV))
    identity = jnp.eye(LEV, dtype=jnp.float32)
    return offdiag * (1.0 - identity) + identity * diag[:, :, None]


def touch_ends(array, stream_key, smallest, top_value):
    dims = array.shape
    index_at = [jax.random.randint(jax.random.fold_in(stream_key, axis), (), 0, dims[axis]) for axis in range(len(dims))]
    array = array.at[tuple(index_at)].set(smallest)
    longest = dims.index(max(dims))
    index_at[longest] = (index_at[longest] + 1) % dims[longest]
    return array.at[tuple(index_at)].set(top_value)


def level_of(own_key, dims, cuts, least, high):
    gain, own = 1.0, jax.random.fold_in(own_key, 6)
    for dim, shards_of in cuts:
        draws = jnp.exp(jax.random.uniform(jax.random.fold_in(own, dim), (shards_of,), jnp.float32, least / len(cuts), high / len(cuts)))
        gain = gain * jnp.repeat(draws, dims[dim] // shards_of).reshape([-1 if axis == dim else 1 for axis in range(len(dims))])
    return gain


def routed_block(rng, own, number, rows, count, top, bound, skew):
    ranking = jax.random.permutation(rng, count)
    crowded, usual = portions_of(count, rows * top, bound, skew, True), portions_of(count, rows * top, bound, skew, False)
    places = jnp.arange(count)

    def named(lengths, rotation):
        used = int((lengths > 0).sum())
        fixed = max(1, used // 4)
        moved = fixed + (places - fixed + rotation * (used - fixed)) % max(1, count - fixed)
        return jnp.zeros((count,), jnp.int32).at[ranking[jnp.where(places < fixed, places, moved)]].set(jnp.asarray(lengths, jnp.int32))

    lengths = jnp.where(number % 4 == 0, named(crowded, number // 4), named(usual, number - number // 4 - 1))
    mixed = jax.random.permutation(jax.random.fold_in(own, 3), count)
    donor, taker = mixed[0:count // 2 * 2:2], mixed[1:count // 2 * 2:2]
    room = jnp.minimum(lengths[donor] - 1, bound - lengths[taker]) // 2
    room = jnp.where((donor == ranking[0]) | (taker == ranking[0]) | (lengths[taker] == 0), 0, jnp.maximum(room, 0))
    moved = jax.random.randint(jax.random.fold_in(own, 4), (count // 2,), 0, 1 << 20) % (room + 1)
    lengths = lengths.at[donor].add(-moved).at[taker].add(moved)
    labels = jnp.searchsorted(jnp.cumsum(lengths), jnp.arange(rows * top), side="right").astype(jnp.int32)
    table = labels.reshape(top, rows).T
    table = table[jax.random.permutation(jax.random.fold_in(own, 1), rows)]
    rotation = jax.random.randint(jax.random.fold_in(own, 2), (rows, 1), 0, top)
    return jnp.take_along_axis(table, (jnp.arange(top)[None, :] + rotation) % top, axis=1)


def portions_of(count, total, most, slope, full):
    weights = [(1 << 20) // math.isqrt(grade ** slope) + 1 for grade in range(1, count + 1)]
    largest = most if full else min(most, max(-(-total // count), total * weights[0] // sum(weights)))
    least = 1 if total - largest >= count - 1 else 0
    given, spare = [largest] + [least] * (count - 1), total - largest - least * (count - 1)
    while spare > 0:
        candidates = [i for i in range(1, count) if given[i] < largest] or [i for i in range(1, count) if given[i] < most]
        whole, remaining = sum([weights[i] for i in candidates]), spare
        for i in candidates:
            extra = min(most - given[i], max(1, remaining * weights[i] // whole), spare)
            given[i] = given[i] + extra
            spare = spare - extra
    return np.array(given)


def scatter_about(rng, extent, scale, reach, cuts=(), kind=jnp.bfloat16):
    array = jax.random.normal(rng, extent, jnp.float32) * scale
    if len(cuts) > 0:
        array = level_of(rng, extent, cuts, -0.22, 0.18) * array
    return jnp.clip(array, min=-reach, max=reach).astype(kind)


def setup_inputs(seed: int = 0) -> dict:
    streams_of = jax.random.split(jax.random.key(seed), 11)
    dual_model = scatter_about(streams_of[0], (SUBS, LEV, NX, NY), 1.0, 6.0, ((0, 8), (2, 16)), jnp.float32)
    state_incr = scatter_about(streams_of[1], (SUBS, LEV, NX, NY), 1.0, 6.0, ((0, 8), (2, 16)), jnp.float32)
    dual_obs = scatter_about(streams_of[2], (SUBS, NBLOCKS, LEV, OB), 1.0, 6.0, ((0, 8), (1, 16)), jnp.float32)
    model_var = jnp.clip(jnp.exp(math.log(2.0) - 2.3025851 * jax.random.uniform(streams_of[3], (SUBS, LEV, NX, NY), jnp.float32) ** level_of(streams_of[3], (SUBS, LEV, NX, NY), ((0, 8), (2, 16)), -0.2, 0.2)), 0.2, 2.0)
    obs_var = jnp.clip(jnp.exp(math.log(2.0) - 2.3025851 * jax.random.uniform(streams_of[4], (SUBS, NBLOCKS, LEV, OB), jnp.float32) ** level_of(streams_of[4], (SUBS, NBLOCKS, LEV, OB), ((0, 8), (1, 16)), -0.2, 0.2)), 0.2, 2.0)
    level_mix = draw_level_mix(jax.random.fold_in(streams_of[10], 71), 0)
    diffusivity = jnp.clip(0.02 + 0.2 * jax.random.uniform(streams_of[6], (SUBS, NX, NY), jnp.float32) ** level_of(streams_of[6], (SUBS, NX, NY), ((0, 8), (1, 16)), -0.2, 0.2), 0.02, 0.22)
    obs_tile_keys = jax.random.split(jax.random.fold_in(streams_of[7], 1), SUBS * NBLOCKS // NB_DEV)
    obs_tile_turns = jax.random.permutation(jax.random.fold_in(streams_of[7], 3), SUBS * NBLOCKS // NB_DEV)
    obs_tile = jax.vmap(lambda own, number: routed_block(jax.random.fold_in(streams_of[7], 2), own, number, NB_DEV, N_SPACE, 1, MOST, 2))(obs_tile_keys, obs_tile_turns).reshape((SUBS, NBLOCKS, 1))
    obs_cells = touch_ends(jax.random.randint(streams_of[8], (SUBS, N_SPACE, N_SPACE, MOST, TAPS, OB), 0, CX * NY), jax.random.fold_in(streams_of[8], 1), 0, (CX * NY) - 1).astype(jnp.int32)
    obs_weights = jnp.clip(0.1 + 0.4 * jax.random.uniform(streams_of[9], (SUBS, N_SPACE, N_SPACE, MOST, TAPS, OB), jnp.float32) ** level_of(streams_of[9], (SUBS, N_SPACE, N_SPACE, MOST, TAPS, OB), ((0, 8), (1, 16)), -0.2, 0.2), 0.1, 0.5)
    return {"dual_model": dual_model, "state_incr": state_incr, "dual_obs": dual_obs, "model_var": model_var, "obs_var": obs_var, "level_mix": level_mix, "diffusivity": diffusivity, "obs_tile": obs_tile, "obs_cells": obs_cells, "obs_weights": obs_weights}


HIGH = lax.Precision.HIGHEST


def laplace(field):
    padded = jnp.pad(field, ((0, 0), (0, 0), (1, 1), (1, 1)))
    center = padded[:, :, 1:-1, 1:-1]
    return (padded[:, :, 2:, 1:-1] + padded[:, :, :-2, 1:-1] + padded[:, :, 1:-1, 2:]
            + padded[:, :, 1:-1, :-2] - 4.0 * center)


def mix_down(level_mix, field):
    return jnp.einsum('slm,smxy->slxy', level_mix, field, precision=HIGH)


def mix_up(level_mix, field):
    return jnp.einsum('sml,smxy->slxy', level_mix, field, precision=HIGH)


def slot_numbers(tiles):
    count = tiles.shape[0]
    same = tiles[:, None] == tiles[None, :]
    earlier = jnp.arange(count)[:, None] > jnp.arange(count)[None, :]
    return jnp.sum((same & earlier).astype(jnp.int32), axis=1).astype(jnp.int32)


def tile_values(grid_tile, cells_tile, weights_tile):
    picked = jnp.take(grid_tile, cells_tile.reshape(-1), axis=1).reshape((LEV,) + cells_tile.shape)
    return jnp.einsum('lostb,ostb->oslb', picked, weights_tile, precision=HIGH)


def tile_adjoint(packed_tile, cells_tile, weights_tile):
    contrib = jnp.einsum('oslb,ostb->lostb', packed_tile, weights_tile, precision=HIGH).reshape(LEV, -1)
    return jnp.zeros((LEV, CX * NY), jnp.float32).at[:, cells_tile.reshape(-1)].add(contrib)


def reference(dual_model, state_incr, dual_obs, model_var, obs_var, level_mix, diffusivity, obs_tile, obs_cells, obs_weights):
    prior = jnp.roll(state_incr, 1, axis=0)
    forward = mix_down(level_mix, prior) + diffusivity[:, None] * laplace(prior)
    model_rows = model_var * dual_model + state_incr - forward
    local_back = mix_up(level_mix, dual_model) + laplace(diffusivity[:, None] * dual_model)
    back = jnp.roll(local_back, -1, axis=0)
    obs_list = []
    adj_list = []
    for window in range(SUBS):
        grid = state_incr[window].reshape(LEV, N_SPACE, CX * NY).transpose(1, 0, 2)
        cells = obs_cells[window]
        weights = obs_weights[window]
        values = jax.vmap(tile_values)(grid, cells, weights)
        tiles = obs_tile[window, :, 0].reshape(N_SPACE, NB_DEV).astype(jnp.int32)
        slots = jax.vmap(slot_numbers)(tiles)
        owners = jnp.broadcast_to(jnp.arange(N_SPACE, dtype=jnp.int32)[:, None], tiles.shape)
        picked = values[tiles, owners, slots]
        obs_list.append(obs_var[window] * dual_obs[window] + picked.reshape(NBLOCKS, LEV, OB))
        packed = jnp.zeros((N_SPACE, N_SPACE, MOST, LEV, OB), jnp.float32)
        packed = packed.at[tiles, owners, slots].set(dual_obs[window].reshape(N_SPACE, NB_DEV, LEV, OB))
        adj = jax.vmap(tile_adjoint)(packed, cells, weights)
        adj_list.append(adj.reshape(N_SPACE, LEV, CX, NY).transpose(1, 0, 2, 3).reshape(LEV, NX, NY))
    obs_rows = jnp.stack(obs_list)
    state_rows = dual_model - back + jnp.stack(adj_list)
    return model_rows, obs_rows, state_rows
```

```python
import functools

import jax
import jax.numpy as jnp
from jax import lax
from jax.experimental import pallas as pl
from jax.experimental.pallas import tpu as pltpu
from jax.sharding import PartitionSpec as P

HIGH = lax.Precision.HIGHEST
F32 = jnp.float32
BF16 = jnp.bfloat16

LEV, CX, NY = 32, 64, 512
SLOTS, TAPS, OB = 64, 4, 128
GROUPS = 4
TROWS = CX * NY // GROUPS
XG = CX // GROUPS
SUBL = 8
NACC = 8
VMEM_LIMIT = 56 << 20


def any_spec():
    return pl.BlockSpec(memory_space=pl.ANY)


def vmem_spec():
    return pl.BlockSpec(memory_space=pltpu.VMEM)


def gather_kernel(rows_hbm, x_hbm, q_ref, w_ref, o_ref, xs, tab, raw0, raw1, idx0, idx1, xsem, isem):
    raws, idxs = (raw0, raw1), (idx0, idx1)

    def fetch(s, par):
        return pltpu.make_async_copy(rows_hbm.at[s], idxs[par], isem.at[par])

    copies = [
        pltpu.make_async_copy(x_hbm.at[:, pl.ds(c * 128, 128)], xs.at[c], xsem.at[c])
        for c in range(4)
    ]
    for copy in copies:
        copy.start()
    fetch(0, 0).start()
    fetch(1, 1).start()
    for c in range(4):
        copies[c].wait()

        @pl.loop(0, XG // 4)
        def _(x4):
            for i in range(4):
                xx = x4 * 4 + i
                block = jnp.concatenate(
                    [xs[c, pl.ds(xx + XG * q, LEV, stride=CX), :] for q in range(GROUPS)], axis=0
                )
                tab[pl.ds(pl.multiple_of(xx * NY + c * 128, 128), 128), :] = block.T

    def finish(s, raw):
        w4, q4 = w_ref[s], q_ref[s]
        total = jnp.zeros((LEV, OB), F32)
        for t in range(TAPS):
            a = raw[t * OB : (t + 1) * OB, :].T
            for q in range(GROUPS):
                total = total + a[q * LEV : (q + 1) * LEV] * jnp.where(
                    q4[t : t + 1] == q, w4[t : t + 1], 0.0
                )
        o_ref[s] = total

    @pl.loop(0, SLOTS // 2)
    def _(pair):
        for par in range(2):
            s = pair * 2 + par
            fetch(s, par).wait()
            finish(jnp.maximum(s - 1, 0), raws[1 - par])
            for t in range(TAPS):
                for b in range(OB):
                    i = idxs[par][t, b]
                    raws[par][t * OB + b : t * OB + b + 1, :] = tab[pl.ds(i, 1), :]

            @pl.when(s + 2 < SLOTS)
            def _():
                fetch(s + 2, par).start()

    finish(SLOTS - 1, raws[1])


def gather(rows, field, quarter, weights):
    return pl.pallas_call(
        gather_kernel,
        out_shape=jax.ShapeDtypeStruct((SLOTS, LEV, OB), F32),
        in_specs=[any_spec(), any_spec(), vmem_spec(), vmem_spec()],
        out_specs=vmem_spec(),
        scratch_shapes=[
            pltpu.VMEM((4, LEV * CX, 128), F32),
            pltpu.VMEM((TROWS, 128), F32),
            pltpu.VMEM((TAPS * OB, 128), F32),
            pltpu.VMEM((TAPS * OB, 128), F32),
            pltpu.SMEM((TAPS, OB), jnp.int32),
            pltpu.SMEM((TAPS, OB), jnp.int32),
            pltpu.SemaphoreType.DMA((4,)),
            pltpu.SemaphoreType.DMA((2,)),
        ],
        compiler_params=pltpu.CompilerParams(vmem_limit_bytes=VMEM_LIMIT),
        cost_estimate=pl.CostEstimate(flops=40_000_000, bytes_accessed=100_000_000, transcendentals=0),
        name="interpolate",
    )(rows, field, quarter, weights)


def scatter_kernel(rows_hbm, d_ref, dual_hbm, q_ref, w_ref, o_hbm, xs, prod0, prod1, idx0, idx1, xsem, isem, *accs):
    prods, idxs = (prod0, prod1), (idx0, idx1)

    def fetch(s, par):
        return pltpu.make_async_copy(rows_hbm.at[s], idxs[par], isem.at[par])

    loads = [
        pltpu.make_async_copy(dual_hbm.at[:, pl.ds(c * 128, 128)], xs.at[c], xsem.at[c])
        for c in range(4)
    ]
    for copy in loads:
        copy.start()
    fetch(0, 0).start()
    fetch(1, 1).start()
    zero = jnp.zeros((64, 128), F32)

    @pl.loop(0, TROWS // 64)
    def _(i):
        for acc in accs:
            acc[pl.ds(pl.multiple_of(i * 64, 64), 64), :] = zero

    def prepare(s, prod):
        w4, q4, d = w_ref[s], q_ref[s], d_ref[s]
        for t in range(TAPS):
            a = jnp.concatenate(
                [d * jnp.where(q4[t : t + 1] == q, w4[t : t + 1], 0.0) for q in range(GROUPS)],
                axis=0,
            )
            prod[t * OB : (t + 1) * OB, :] = a.T

    prepare(0, prods[0])
    per = NACC // TAPS

    @pl.loop(0, SLOTS // 2)
    def _(pair):
        for par in range(2):
            s = pair * 2 + par
            fetch(s, par).wait()
            prepare(jnp.minimum(s + 1, SLOTS - 1), prods[1 - par])
            for g in range(OB // per):
                news = []
                for j in range(per):
                    for t in range(TAPS):
                        b = g * per + j
                        i = idxs[par][t, b]
                        new = accs[j * TAPS + t][pl.ds(i, 1), :] + prods[par][t * OB + b : t * OB + b + 1, :]
                        news.append((i, new))
                for k, (i, new) in enumerate(news):
                    accs[k][pl.ds(i, 1), :] = new

            @pl.when(s + 2 < SLOTS)
            def _():
                fetch(s + 2, par).start()

    stores = [
        pltpu.make_async_copy(xs.at[c], o_hbm.at[:, pl.ds(c * 128, 128)], xsem.at[c])
        for c in range(4)
    ]
    for c in range(4):
        loads[c].wait()

        @pl.loop(0, XG // 4)
        def _(x4):
            for i in range(4):
                xx = x4 * 4 + i
                at = pl.ds(pl.multiple_of(xx * NY + c * 128, 128), 128)
                total = accs[0][at, :]
                for acc in accs[1:]:
                    total = total + acc[at, :]
                back = total.T
                for q in range(GROUPS):
                    to = pl.ds(xx + XG * q, LEV, stride=CX)
                    xs[c, to, :] = xs[c, to, :] + back[q * LEV : (q + 1) * LEV]

        stores[c].start()
    for copy in stores:
        copy.wait()


def scatter(rows, packed, dual, quarter, weights):
    return pl.pallas_call(
        scatter_kernel,
        out_shape=jax.ShapeDtypeStruct((LEV * CX, NY), F32),
        in_specs=[any_spec(), vmem_spec(), any_spec(), vmem_spec(), vmem_spec()],
        out_specs=any_spec(),
        scratch_shapes=[
            pltpu.VMEM((4, LEV * CX, 128), F32),
            pltpu.VMEM((TAPS * OB, 128), F32),
            pltpu.VMEM((TAPS * OB, 128), F32),
            pltpu.SMEM((TAPS, OB), jnp.int32),
            pltpu.SMEM((TAPS, OB), jnp.int32),
            pltpu.SemaphoreType.DMA((4,)),
            pltpu.SemaphoreType.DMA((2,)),
        ]
        + [pltpu.VMEM((TROWS, 128), F32)] * NACC,
        compiler_params=pltpu.CompilerParams(vmem_limit_bytes=VMEM_LIMIT),
        cost_estimate=pl.CostEstimate(flops=40_000_000, bytes_accessed=120_000_000, transcendentals=0),
        name="spread",
    )(rows, packed, dual, quarter, weights)


def split(a):
    high = a.astype(BF16)
    return high, (a - high.astype(F32)).astype(BF16)


def mixed(mix, field):
    mh, ml = split(mix)
    fh, fl = split(field.reshape(LEV * SUBL, NY))
    dot = functools.partial(jnp.dot, preferred_element_type=F32)
    return (dot(mh, fh) + (dot(mh, fl) + dot(ml, fh))).reshape(LEV, SUBL, NY)


def laplace(low, field, high):
    row = lax.broadcasted_iota(jnp.int32, field.shape, 1)
    col = lax.broadcasted_iota(jnp.int32, field.shape, 2)
    flat = field.reshape(LEV * SUBL, NY)
    left = pltpu.roll(flat, 1, 1).reshape(field.shape)
    right = pltpu.roll(flat, NY - 1, 1).reshape(field.shape)
    up = pltpu.roll(field, 1, 1)
    down = pltpu.roll(field, SUBL - 1, 1)
    up = jnp.where(row == 0, low, up)
    down = jnp.where(row == SUBL - 1, high, down)
    left = jnp.where(col == 0, 0.0, left)
    right = jnp.where(col == NY - 1, 0.0, right)
    return (up + down) + (left + right) - 4.0 * field


def lagged(step, steps, cur_ref, lo_ref, hi_ref, mid, low):
    @pl.when(step == 1)
    def _():
        low[...] = lo_ref[...]

    cur = cur_ref[0]
    high = jnp.where(step == steps - 1, hi_ref[...], cur[:, 0:1, :])
    return low[...], mid[...], high, cur


def model_kernel(steps, mix_ref, p_ref, lo_ref, hi_ref, diff_ref, var_ref, dual_ref, x_ref, o_ref, mid, low):
    step = pl.program_id(0)
    before, block, after, cur = lagged(step, steps, p_ref, lo_ref, hi_ref, mid, low)

    @pl.when(step > 0)
    def _():
        forward = mixed(mix_ref[...], block) + diff_ref[0][None] * laplace(before, block, after)
        o_ref[0] = var_ref[0] * dual_ref[0] + x_ref[0] - forward
        low[...] = block[:, SUBL - 1 : SUBL, :]

    mid[...] = cur


def adjoint_kernel(steps, mix_ref, d_ref, lo_ref, hi_ref, diff_ref, dlag_ref, o_ref, mid, low):
    step = pl.program_id(0)
    scaled = d_ref[...] * diff_ref[...][:, None]
    before, block, after, cur = lagged(step, steps, scaled, lo_ref, hi_ref, mid, low)

    @pl.when(step > 0)
    def _():
        o_ref[0] = mixed(mix_ref[...], dlag_ref[0]) + laplace(before, block, after)
        low[...] = block[:, SUBL - 1 : SUBL, :]

    mid[...] = cur


STEPS = CX // SUBL + 1


def field_spec(lag):
    if lag:
        return pl.BlockSpec((1, LEV, SUBL, NY), lambda g: (0, 0, jnp.maximum(g - 1, 0), 0))
    return pl.BlockSpec((1, LEV, SUBL, NY), lambda g: (0, 0, jnp.minimum(g, STEPS - 2), 0))


def diff_spec(lag):
    if lag:
        return pl.BlockSpec((1, SUBL, NY), lambda g: (0, jnp.maximum(g - 1, 0), 0))
    return pl.BlockSpec((1, SUBL, NY), lambda g: (0, jnp.minimum(g, STEPS - 2), 0))


def whole_spec(shape):
    return pl.BlockSpec(shape, lambda g: (0,) * len(shape))


def stencil_call(kernel, in_specs, name):
    return pl.pallas_call(
        functools.partial(kernel, STEPS),
        out_shape=jax.ShapeDtypeStruct((1, LEV, CX, NY), F32),
        grid=(STEPS,),
        in_specs=in_specs,
        out_specs=field_spec(True),
        scratch_shapes=[pltpu.VMEM((LEV, SUBL, NY), F32), pltpu.VMEM((LEV, 1, NY), F32)],
        compiler_params=pltpu.CompilerParams(vmem_limit_bytes=VMEM_LIMIT),
        cost_estimate=pl.CostEstimate(flops=2_000_000_000, bytes_accessed=20_000_000, transcendentals=0),
        name=name,
    )


def model_rows_of(mix, prior, lo, hi, diff, var, dual, x):
    edge = whole_spec((LEV, 1, NY))
    return stencil_call(
        model_kernel,
        [whole_spec((LEV * SUBL, LEV * SUBL)), field_spec(False), edge, edge, diff_spec(True)]
        + [field_spec(True)] * 3,
        "model",
    )(mix, prior, lo, hi, diff, var, dual, x)


def adjoint_of(mix, dual, lo, hi, diff):
    edge = whole_spec((LEV, 1, NY))
    return stencil_call(
        adjoint_kernel,
        [whole_spec((LEV * SUBL, LEV * SUBL)), field_spec(False), edge, edge, diff_spec(False), field_spec(True)],
        "adjoint",
    )(mix, dual, lo, hi, diff, dual)


def moved(block, dtm, dspace):
    ntm, nspace = lax.axis_size("tm"), lax.axis_size("space")
    pairs = [
        (t * nspace + s, ((t + dtm) % ntm) * nspace + s + dspace)
        for t in range(ntm)
        for s in range(nspace)
        if 0 <= s + dspace < nspace
    ]
    return lax.ppermute(block, ("tm", "space"), pairs)


def on_device(
    dual_model,
    state_incr,
    dual_obs,
    model_var,
    obs_var,
    level_mix,
    diffusivity,
    obs_tile,
    obs_cells,
    obs_weights,
):
    ntiles = lax.axis_size("space")
    capacity = obs_cells.shape[3]

    first, last = diffusivity[0, 0:1, :], diffusivity[0, CX - 1 : CX, :]
    adj_lo = moved(last[None] * dual_model[0, :, CX - 1 : CX, :], 0, 1)
    adj_hi = moved(first[None] * dual_model[0, :, 0:1, :], 0, -1)
    pri_lo = moved(state_incr[0, :, CX - 1 : CX, :], 1, 1)
    pri_hi = moved(state_incr[0, :, 0:1, :], 1, -1)

    tiles = obs_tile[0, :, 0]
    nblock = tiles.shape[0]
    same = tiles[:, None] == tiles[None, :]
    earlier = jnp.arange(nblock)[:, None] > jnp.arange(nblock)[None, :]
    slots = jnp.sum((same & earlier).astype(jnp.int32), axis=1)
    slot_pos = tiles * capacity + slots
    onehot = (slot_pos[:, None] == jnp.arange(ntiles * capacity, dtype=jnp.int32)[None, :]).astype(F32)
    packed = jnp.dot(onehot.T, dual_obs[0].reshape(nblock, LEV * OB), precision=HIGH)
    packed = packed.reshape(ntiles * capacity, LEV, OB)
    got_dual = lax.all_to_all(packed, "space", split_axis=0, concat_axis=0, tiled=True)

    cells = obs_cells.reshape(SLOTS, TAPS, OB)
    weights = obs_weights.reshape(SLOTS, TAPS, OB)
    rows, quarter = cells & (TROWS - 1), lax.shift_right_logical(cells, 13)

    prior = moved(state_incr, 1, 0)
    eye = jnp.eye(SUBL, dtype=F32)
    wide = (level_mix[0][:, None, :, None] * eye[None, :, None, :]).reshape(LEV * SUBL, LEV * SUBL)
    wide_t = (level_mix[0].T[:, None, :, None] * eye[None, :, None, :]).reshape(LEV * SUBL, LEV * SUBL)
    back = moved(adjoint_of(wide_t, dual_model, adj_lo, adj_hi, diffusivity), -1, 0)

    interp = gather(rows, state_incr.reshape(LEV * CX, NY), quarter, weights)
    got_dual, interp = lax.optimization_barrier((got_dual, interp))
    got_interp = lax.all_to_all(interp, "space", split_axis=0, concat_axis=0, tiled=True)
    with_obs = scatter(rows, got_dual, dual_model.reshape(LEV * CX, NY), quarter, weights)

    model_rows = model_rows_of(wide, prior, pri_lo, pri_hi, diffusivity, model_var, dual_model, state_incr)
    state_rows = with_obs.reshape(1, LEV, CX, NY) - back
    flat_interp = got_interp.reshape(ntiles * capacity, LEV * OB)
    mine = jnp.dot(onehot, flat_interp, precision=HIGH).reshape(1, nblock, LEV, OB)
    obs_rows = obs_var * dual_obs + mine
    return (model_rows, obs_rows, state_rows)


def solution(mesh):
    field = P("tm", None, "space", None)
    blocks = P("tm", "space", None, None)
    taps = P("tm", "space", None, None, None, None)
    placed = (
        field,
        field,
        blocks,
        field,
        blocks,
        P("tm", None, None),
        P("tm", "space", None),
        P("tm", "space", None),
        taps,
        taps,
    )
    return jax.shard_map(
        on_device,
        mesh=mesh,
        in_specs=placed,
        out_specs=(field, blocks, field),
        check_vma=False,
    )
```

```python
import functools

import jax
import jax.numpy as jnp
from jax import lax
from jax.experimental import pallas as pl
from jax.experimental.pallas import tpu as pltpu
from jax.sharding import PartitionSpec as P

HIGH = lax.Precision.HIGHEST
F32 = jnp.float32
BF16 = jnp.bfloat16

LEV, CX, NY = 32, 64, 512
SLOTS, TAPS, OB = 64, 4, 128
GROUPS = 4
TROWS = CX * NY // GROUPS
XG = CX // GROUPS
SUBL = 8
NACC = 8
RING = 4
VMEM_LIMIT = 56 << 20


def any_spec():
    return pl.BlockSpec(memory_space=pl.ANY)


def vmem_spec():
    return pl.BlockSpec(memory_space=pltpu.VMEM)


def gather_kernel(rows_ref, x_hbm, q_ref, w_ref, o_ref, xs, tab, raw0, raw1, xsem, isem, *idxs):
    raws = (raw0, raw1)

    def fetch(s, par):
        return pltpu.make_async_copy(rows_ref.at[s], idxs[par], isem.at[par])

    copies = [
        pltpu.make_async_copy(x_hbm.at[:, pl.ds(c * 128, 128)], xs.at[c], xsem.at[c])
        for c in range(4)
    ]
    for copy in copies:
        copy.start()
    for r in range(RING):
        fetch(r, r).start()
    for c in range(4):
        copies[c].wait()

        @pl.loop(0, XG // 4)
        def _(x4):
            for i in range(4):
                xx = x4 * 4 + i
                block = jnp.concatenate(
                    [xs[c, pl.ds(xx + XG * q, LEV, stride=CX), :] for q in range(GROUPS)], axis=0
                )
                tab[pl.ds(pl.multiple_of(xx * NY + c * 128, 128), 128), :] = block.T

    def finish(s, raw):
        w4, q4 = w_ref[s], q_ref[s]
        total = jnp.zeros((LEV, OB), F32)
        for t in range(TAPS):
            a = raw[t * OB : (t + 1) * OB, :].T
            for q in range(GROUPS):
                total = total + a[q * LEV : (q + 1) * LEV] * jnp.where(
                    q4[t : t + 1] == q, w4[t : t + 1], 0.0
                )
        o_ref[s] = total

    @pl.loop(0, SLOTS // RING)
    def _(group):
        for r in range(RING):
            s, par = group * RING + r, r % 2
            fetch(s, r).wait()
            finish(jnp.maximum(s - 1, 0), raws[1 - par])
            for t in range(TAPS):
                for b in range(OB):
                    i = idxs[r][t, b]
                    raws[par][t * OB + b : t * OB + b + 1, :] = tab[pl.ds(i, 1), :]

            @pl.when(s + RING < SLOTS)
            def _():
                fetch(s + RING, r).start()

    finish(SLOTS - 1, raws[1])


def gather(rows, field, quarter, weights):
    return pl.pallas_call(
        gather_kernel,
        out_shape=jax.ShapeDtypeStruct((SLOTS, LEV, OB), F32),
        in_specs=[vmem_spec(), any_spec(), vmem_spec(), vmem_spec()],
        out_specs=vmem_spec(),
        scratch_shapes=[
            pltpu.VMEM((4, LEV * CX, 128), F32),
            pltpu.VMEM((TROWS, 128), F32),
            pltpu.VMEM((TAPS * OB, 128), F32),
            pltpu.VMEM((TAPS * OB, 128), F32),
            pltpu.SemaphoreType.DMA((4,)),
            pltpu.SemaphoreType.DMA((RING,)),
        ]
        + [pltpu.SMEM((TAPS, OB), jnp.int32)] * RING,
        compiler_params=pltpu.CompilerParams(vmem_limit_bytes=VMEM_LIMIT),
        cost_estimate=pl.CostEstimate(flops=40_000_000, bytes_accessed=100_000_000, transcendentals=0),
        name="interpolate",
    )(rows, field, quarter, weights)


def scatter_kernel(rows_ref, d_ref, dual_hbm, q_ref, w_ref, o_hbm, xs, prod0, prod1, xsem, isem, *rest):
    prods, idxs, accs = (prod0, prod1), rest[:RING], rest[RING:]

    def fetch(s, par):
        return pltpu.make_async_copy(rows_ref.at[s], idxs[par], isem.at[par])

    loads = [
        pltpu.make_async_copy(dual_hbm.at[:, pl.ds(c * 128, 128)], xs.at[c], xsem.at[c])
        for c in range(4)
    ]
    for copy in loads:
        copy.start()
    for r in range(RING):
        fetch(r, r).start()
    zero = jnp.zeros((64, 128), F32)

    @pl.loop(0, TROWS // 64)
    def _(i):
        for acc in accs:
            acc[pl.ds(pl.multiple_of(i * 64, 64), 64), :] = zero

    def prepare(s, prod):
        w4, q4, d = w_ref[s], q_ref[s], d_ref[s]
        for t in range(TAPS):
            a = jnp.concatenate(
                [d * jnp.where(q4[t : t + 1] == q, w4[t : t + 1], 0.0) for q in range(GROUPS)],
                axis=0,
            )
            prod[t * OB : (t + 1) * OB, :] = a.T

    prepare(0, prods[0])
    per = NACC // TAPS

    @pl.loop(0, SLOTS // RING)
    def _(group):
        for r in range(RING):
            s, par = group * RING + r, r % 2
            fetch(s, r).wait()
            prepare(jnp.minimum(s + 1, SLOTS - 1), prods[1 - par])
            for g in range(OB // per):
                news = []
                for j in range(per):
                    for t in range(TAPS):
                        b = g * per + j
                        i = idxs[r][t, b]
                        new = accs[j * TAPS + t][pl.ds(i, 1), :] + prods[par][t * OB + b : t * OB + b + 1, :]
                        news.append((i, new))
                for k, (i, new) in enumerate(news):
                    accs[k][pl.ds(i, 1), :] = new

            @pl.when(s + RING < SLOTS)
            def _():
                fetch(s + RING, r).start()

    stores = [
        pltpu.make_async_copy(xs.at[c], o_hbm.at[:, pl.ds(c * 128, 128)], xsem.at[c])
        for c in range(4)
    ]
    for c in range(4):
        loads[c].wait()

        @pl.loop(0, XG // 4)
        def _(x4):
            for i in range(4):
                xx = x4 * 4 + i
                at = pl.ds(pl.multiple_of(xx * NY + c * 128, 128), 128)
                total = accs[0][at, :]
                for acc in accs[1:]:
                    total = total + acc[at, :]
                back = total.T
                for q in range(GROUPS):
                    to = pl.ds(xx + XG * q, LEV, stride=CX)
                    xs[c, to, :] = xs[c, to, :] + back[q * LEV : (q + 1) * LEV]

        stores[c].start()
    for copy in stores:
        copy.wait()


def scatter(rows, packed, dual, quarter, weights):
    return pl.pallas_call(
        scatter_kernel,
        out_shape=jax.ShapeDtypeStruct((LEV * CX, NY), F32),
        in_specs=[vmem_spec(), vmem_spec(), any_spec(), vmem_spec(), vmem_spec()],
        out_specs=any_spec(),
        scratch_shapes=[
            pltpu.VMEM((4, LEV * CX, 128), F32),
            pltpu.VMEM((TAPS * OB, 128), F32),
            pltpu.VMEM((TAPS * OB, 128), F32),
            pltpu.SemaphoreType.DMA((4,)),
            pltpu.SemaphoreType.DMA((RING,)),
        ]
        + [pltpu.SMEM((TAPS, OB), jnp.int32)] * RING
        + [pltpu.VMEM((TROWS, 128), F32)] * NACC,
        compiler_params=pltpu.CompilerParams(vmem_limit_bytes=VMEM_LIMIT),
        cost_estimate=pl.CostEstimate(flops=40_000_000, bytes_accessed=120_000_000, transcendentals=0),
        name="spread",
    )(rows, packed, dual, quarter, weights)


def split(a):
    high = a.astype(BF16)
    return high, (a - high.astype(F32)).astype(BF16)


DOT = functools.partial(lax.dot_general, preferred_element_type=F32)
PLAIN, BY_ROWS = (((1,), (0,)), ((), ())), (((1,), (1,)), ((), ()))
WIDE = LEV * SUBL
STEPS = CX // SUBL + 1


def widen(mix_ref, wide, transposed):
    row = lax.broadcasted_iota(jnp.int32, (WIDE, LEV), 0)
    col = lax.broadcasted_iota(jnp.int32, (WIDE, LEV), 1)
    spread = jnp.where(row // SUBL == col, 1.0, 0.0).astype(BF16)
    rows = lax.broadcasted_iota(jnp.int32, (WIDE, WIDE), 0)
    cols = lax.broadcasted_iota(jnp.int32, (WIDE, WIDE), 1)
    same = rows % SUBL == cols % SUBL
    for h, part in enumerate(split(mix_ref[0])):
        half = DOT(spread, part, BY_ROWS if transposed else PLAIN).astype(BF16)
        wide[h] = jnp.where(same, DOT(half, spread, BY_ROWS), 0.0).astype(BF16)


def mix_into(out, wide, field):
    high, low = split(field)
    mh, ml = wide[0], wide[1]
    out[...] = DOT(mh, high, PLAIN) + (DOT(mh, low, PLAIN) + DOT(ml, high, PLAIN))


def laplace_at(ring, slots, level, row, col):
    before, cur, after = (ring[slot, level] for slot in slots)
    up = pltpu.roll(jnp.where(row == SUBL - 1, before, cur), 1, 0)
    down = pltpu.roll(jnp.where(row == 0, after, cur), SUBL - 1, 0)
    left = jnp.where(col == 0, 0.0, pltpu.roll(cur, 1, 1))
    right = jnp.where(col == NY - 1, 0.0, pltpu.roll(cur, NY - 1, 1))
    return (up + down) + (left + right) - 4.0 * cur


def fill(step, ring, lo_ref, hi_ref, scale_ref, src_ref):
    @pl.when(step == 0)
    def _():
        for level in range(LEV):
            ring[2, level] = jnp.broadcast_to(lo_ref[level], (SUBL, NY))

    @pl.when(step < STEPS - 1)
    def _():
        for level in range(LEV):
            block = src_ref[0, level]
            ring[lax.rem(step, 3), level] = block if scale_ref is None else block * scale_ref[0]

    @pl.when(step == STEPS - 1)
    def _():
        for level in range(LEV):
            ring[lax.rem(step, 3), level] = jnp.broadcast_to(hi_ref[level], (SUBL, NY))


def slots_of(step):
    return lax.rem(step + 1, 3), lax.rem(step + 2, 3), lax.rem(step, 3)


def final_kernel(mix_ref, p_ref, lo_ref, hi_ref, diff_ref, base_ref, obs_ref, back_ref, o_ref, s_ref, ring, mixes, wide):
    step = pl.program_id(0)

    @pl.when(step == 0)
    def _():
        widen(mix_ref, wide, False)

    fill(step, ring, lo_ref, hi_ref, None, p_ref)

    @pl.when(step > 0)
    def _():
        row = lax.broadcasted_iota(jnp.int32, (SUBL, NY), 0)
        col = lax.broadcasted_iota(jnp.int32, (SUBL, NY), 1)
        slots, old = slots_of(step), lax.rem(step + 1, 2)
        diff = diff_ref[0]
        for level in range(LEV):
            mix = mixes[old, level * SUBL : (level + 1) * SUBL, :]
            o_ref[0, level] = base_ref[0, level] - (mix + diff * laplace_at(ring, slots, level, row, col))
            s_ref[0, level] = obs_ref[0, level] - back_ref[0, level]

    @pl.when(step < STEPS - 1)
    def _():
        mix_into(mixes.at[lax.rem(step, 2)], wide, p_ref[0].reshape(WIDE, NY))


def adjoint_kernel(mix_ref, d_ref, lo_ref, hi_ref, diff_ref, o_ref, ring, mixes, wide):
    step = pl.program_id(0)

    @pl.when(step == 0)
    def _():
        widen(mix_ref, wide, True)

    fill(step, ring, lo_ref, hi_ref, diff_ref, d_ref)

    @pl.when(step > 0)
    def _():
        row = lax.broadcasted_iota(jnp.int32, (SUBL, NY), 0)
        col = lax.broadcasted_iota(jnp.int32, (SUBL, NY), 1)
        slots, old = slots_of(step), lax.rem(step + 1, 2)
        for level in range(LEV):
            mix = mixes[old, level * SUBL : (level + 1) * SUBL, :]
            o_ref[0, level] = mix + laplace_at(ring, slots, level, row, col)

    @pl.when(step < STEPS - 1)
    def _():
        mix_into(mixes.at[lax.rem(step, 2)], wide, d_ref[0].reshape(WIDE, NY))


def now_or_before(before, shape, dim):
    def at(g):
        place = jnp.maximum(g - 1, 0) if before else jnp.minimum(g, STEPS - 2)
        return tuple(place if d == dim else 0 for d in range(len(shape)))

    return pl.BlockSpec(shape, at)


def whole_spec(shape):
    return pl.BlockSpec(shape, lambda g: (0,) * len(shape))


NOW = functools.partial(now_or_before, False)
BEFORE = functools.partial(now_or_before, True)
BLOCK, DIFF = ((1, LEV, SUBL, NY), 2), ((1, SUBL, NY), 1)
EDGE, MIX = (LEV, 1, NY), (1, LEV, LEV)


def stencil_call(kernel, in_specs, outs, moved_bytes, name):
    return pl.pallas_call(
        kernel,
        out_shape=[jax.ShapeDtypeStruct((1, LEV, CX, NY), F32)] * outs,
        grid=(STEPS,),
        in_specs=in_specs,
        out_specs=[BEFORE(*BLOCK)] * outs,
        scratch_shapes=[
            pltpu.VMEM((3, LEV, SUBL, NY), F32),
            pltpu.VMEM((2, WIDE, NY), F32),
            pltpu.VMEM((2, WIDE, WIDE), BF16),
        ],
        compiler_params=pltpu.CompilerParams(vmem_limit_bytes=VMEM_LIMIT),
        cost_estimate=pl.CostEstimate(flops=2_000_000_000, bytes_accessed=moved_bytes, transcendentals=0),
        name=name,
    )


def final_of(mix, prior, lo, hi, diff, base, with_obs, back):
    return stencil_call(
        final_kernel,
        [whole_spec(MIX), NOW(*BLOCK), whole_spec(EDGE), whole_spec(EDGE), BEFORE(*DIFF)] + [BEFORE(*BLOCK)] * 3,
        2,
        24_000_000,
        "final",
    )(mix, prior, lo, hi, diff, base, with_obs, back)


def adjoint_of(mix, dual, lo, hi, diff):
    return stencil_call(
        adjoint_kernel,
        [whole_spec(MIX), NOW(*BLOCK), whole_spec(EDGE), whole_spec(EDGE), NOW(*DIFF)],
        1,
        20_000_000,
        "adjoint",
    )(mix, dual, lo, hi, diff)[0]


def moved(block, dtm, dspace):
    ntm, nspace = lax.axis_size("tm"), lax.axis_size("space")
    pairs = [
        (t * nspace + s, ((t + dtm) % ntm) * nspace + s + dspace)
        for t in range(ntm)
        for s in range(nspace)
        if 0 <= s + dspace < nspace
    ]
    return lax.ppermute(block, ("tm", "space"), pairs)


def on_device(
    dual_model,
    state_incr,
    dual_obs,
    model_var,
    obs_var,
    level_mix,
    diffusivity,
    obs_tile,
    obs_cells,
    obs_weights,
):
    ntiles = lax.axis_size("space")
    capacity = obs_cells.shape[3]

    first, last = diffusivity[0, 0:1, :], diffusivity[0, CX - 1 : CX, :]
    adj_lo = moved(last[None] * dual_model[0, :, CX - 1 : CX, :], 0, 1)
    adj_hi = moved(first[None] * dual_model[0, :, 0:1, :], 0, -1)
    pri_lo = moved(state_incr[0, :, CX - 1 : CX, :], 1, 1)
    pri_hi = moved(state_incr[0, :, 0:1, :], 1, -1)

    tiles = obs_tile[0, :, 0]
    nblock = tiles.shape[0]
    same = tiles[:, None] == tiles[None, :]
    earlier = jnp.arange(nblock)[:, None] > jnp.arange(nblock)[None, :]
    slots = jnp.sum((same & earlier).astype(jnp.int32), axis=1)
    slot_pos = tiles * capacity + slots
    onehot = (slot_pos[:, None] == jnp.arange(ntiles * capacity, dtype=jnp.int32)[None, :]).astype(F32)
    packed = jnp.dot(onehot.T, dual_obs[0].reshape(nblock, LEV * OB), precision=HIGH)
    packed = packed.reshape(ntiles * capacity, LEV, OB)
    packed, adj_lo, adj_hi = lax.optimization_barrier((packed, adj_lo, adj_hi))
    got_dual = lax.all_to_all(packed, "space", split_axis=0, concat_axis=0, tiled=True)

    cells = obs_cells.reshape(SLOTS, TAPS, OB)
    weights = obs_weights.reshape(SLOTS, TAPS, OB)
    rows, quarter = cells & (TROWS - 1), lax.shift_right_logical(cells, 13)

    adjoint = adjoint_of(level_mix, dual_model, adj_lo, adj_hi, diffusivity)
    sent, adjoint, got_dual, pri_lo, pri_hi, field = lax.optimization_barrier(
        (state_incr, adjoint, got_dual, pri_lo, pri_hi, state_incr)
    )
    prior = moved(sent, 1, 0)
    back = moved(adjoint, -1, 0)

    interp = gather(rows, field.reshape(LEV * CX, NY), quarter, weights)
    interp, got_dual = lax.optimization_barrier((interp, got_dual))
    got_interp = lax.all_to_all(interp, "space", split_axis=0, concat_axis=0, tiled=True)
    with_obs = scatter(rows, got_dual, dual_model.reshape(LEV * CX, NY), quarter, weights)

    with_obs, var = lax.optimization_barrier((with_obs, model_var))
    base = var * dual_model + state_incr
    base, with_obs, prior = lax.optimization_barrier((base, with_obs, prior))
    model_rows, state_rows = final_of(
        level_mix, prior, pri_lo, pri_hi, diffusivity, base, with_obs.reshape(1, LEV, CX, NY), back
    )
    flat_interp = got_interp.reshape(ntiles * capacity, LEV * OB)
    mine = jnp.dot(onehot, flat_interp, precision=HIGH).reshape(1, nblock, LEV, OB)
    obs_rows = obs_var * dual_obs + mine
    return (model_rows, obs_rows, state_rows)


def solution(mesh):
    field = P("tm", None, "space", None)
    blocks = P("tm", "space", None, None)
    taps = P("tm", "space", None, None, None, None)
    placed = (
        field,
        field,
        blocks,
        field,
        blocks,
        P("tm", None, None),
        P("tm", "space", None),
        P("tm", "space", None),
        taps,
        taps,
    )
    return jax.shard_map(
        on_device,
        mesh=mesh,
        in_specs=placed,
        out_specs=(field, blocks, field),
        check_vma=False,
    )
```

```python
import functools

import jax
import jax.numpy as jnp
from jax import lax
from jax.experimental import pallas as pl
from jax.experimental.pallas import tpu as pltpu
from jax.sharding import PartitionSpec as P

HIGH = lax.Precision.HIGHEST
F32 = jnp.float32
BF16 = jnp.bfloat16

LEV, CX, NY = 32, 64, 512
SLOTS, TAPS, OB = 64, 4, 128
NBLOCK, MOST = 24, 4
GROUPS = 4
TROWS = CX * NY // GROUPS
XG = CX // GROUPS
SUBL = 8
NACC = 8
VMEM_LIMIT = 60 << 20
RING = 4


def any_spec():
    return pl.BlockSpec(memory_space=pl.ANY)


def vmem_spec():
    return pl.BlockSpec(memory_space=pltpu.VMEM)


def gather_kernel(rows_ref, x_hbm, q_ref, w_ref, o_ref, xs, tab, raw0, raw1, xsem, isem, *idxs):
    raws = (raw0, raw1)

    def fetch(s, par):
        return pltpu.make_async_copy(rows_ref.at[s], idxs[par], isem.at[par])

    copies = [
        pltpu.make_async_copy(x_hbm.at[:, pl.ds(c * 128, 128)], xs.at[c], xsem.at[c])
        for c in range(4)
    ]
    for copy in copies:
        copy.start()
    for r in range(RING):
        fetch(r, r).start()
    for c in range(4):
        copies[c].wait()

        @pl.loop(0, XG // 4)
        def _(x4):
            for i in range(4):
                xx = x4 * 4 + i
                block = jnp.concatenate(
                    [xs[c, pl.ds(xx + XG * q, LEV, stride=CX), :] for q in range(GROUPS)], axis=0
                )
                tab[pl.ds(pl.multiple_of(xx * NY + c * 128, 128), 128), :] = block.T

    def finish(s, raw):
        w4, q4 = w_ref[s], q_ref[s]
        total = jnp.zeros((LEV, OB), F32)
        for t in range(TAPS):
            a = raw[t * OB : (t + 1) * OB, :].T
            for q in range(GROUPS):
                total = total + a[q * LEV : (q + 1) * LEV] * jnp.where(
                    q4[t : t + 1] == q, w4[t : t + 1], 0.0
                )
        o_ref[s] = total

    @pl.loop(0, SLOTS // RING)
    def _(group):
        for r in range(RING):
            s, par = group * RING + r, r % 2
            fetch(s, r).wait()
            finish(jnp.maximum(s - 1, 0), raws[1 - par])
            for t in range(TAPS):
                for b in range(OB):
                    i = idxs[r][t, b]
                    raws[par][t * OB + b : t * OB + b + 1, :] = tab[pl.ds(i, 1), :]

            @pl.when(s + RING < SLOTS)
            def _():
                fetch(s + RING, r).start()

    finish(SLOTS - 1, raws[1])


def gather(rows, field, quarter, weights):
    return pl.pallas_call(
        gather_kernel,
        out_shape=jax.ShapeDtypeStruct((SLOTS, LEV, OB), F32),
        in_specs=[vmem_spec(), any_spec(), vmem_spec(), vmem_spec()],
        out_specs=vmem_spec(),
        scratch_shapes=[
            pltpu.VMEM((4, LEV * CX, 128), F32),
            pltpu.VMEM((TROWS, 128), F32),
            pltpu.VMEM((TAPS * OB, 128), F32),
            pltpu.VMEM((TAPS * OB, 128), F32),
            pltpu.SemaphoreType.DMA((4,)),
            pltpu.SemaphoreType.DMA((RING,)),
        ]
        + [pltpu.SMEM((TAPS, OB), jnp.int32)] * RING,
        compiler_params=pltpu.CompilerParams(vmem_limit_bytes=VMEM_LIMIT),
        cost_estimate=pl.CostEstimate(flops=40_000_000, bytes_accessed=100_000_000, transcendentals=0),
        name="interpolate",
    )(rows, field, quarter, weights)


def scatter_kernel(rows_ref, d_ref, dual_hbm, q_ref, w_ref, o_hbm, xs, prod0, prod1, xsem, isem, *rest):
    prods, idxs, accs = (prod0, prod1), rest[:RING], rest[RING:]

    def fetch(s, par):
        return pltpu.make_async_copy(rows_ref.at[s], idxs[par], isem.at[par])

    loads = [
        pltpu.make_async_copy(dual_hbm.at[:, pl.ds(c * 128, 128)], xs.at[c], xsem.at[c])
        for c in range(4)
    ]
    for copy in loads:
        copy.start()
    for r in range(RING):
        fetch(r, r).start()
    zero = jnp.zeros((64, 128), F32)

    @pl.loop(0, TROWS // 64)
    def _(i):
        for acc in accs:
            acc[pl.ds(pl.multiple_of(i * 64, 64), 64), :] = zero

    def prepare(s, prod):
        w4, q4, d = w_ref[s], q_ref[s], d_ref[s]
        for t in range(TAPS):
            a = jnp.concatenate(
                [d * jnp.where(q4[t : t + 1] == q, w4[t : t + 1], 0.0) for q in range(GROUPS)],
                axis=0,
            )
            prod[t * OB : (t + 1) * OB, :] = a.T

    prepare(0, prods[0])
    per = NACC // TAPS

    @pl.loop(0, SLOTS // RING)
    def _(group):
        for r in range(RING):
            s, par = group * RING + r, r % 2
            fetch(s, r).wait()
            prepare(jnp.minimum(s + 1, SLOTS - 1), prods[1 - par])
            for g in range(OB // per):
                news = []
                for j in range(per):
                    for t in range(TAPS):
                        b = g * per + j
                        i = idxs[r][t, b]
                        new = accs[j * TAPS + t][pl.ds(i, 1), :] + prods[par][t * OB + b : t * OB + b + 1, :]
                        news.append((i, new))
                for k, (i, new) in enumerate(news):
                    accs[k][pl.ds(i, 1), :] = new

            @pl.when(s + RING < SLOTS)
            def _():
                fetch(s + RING, r).start()

    stores = [
        pltpu.make_async_copy(xs.at[c], o_hbm.at[:, pl.ds(c * 128, 128)], xsem.at[c])
        for c in range(4)
    ]
    for c in range(4):
        loads[c].wait()

        @pl.loop(0, XG // 4)
        def _(x4):
            for i in range(4):
                xx = x4 * 4 + i
                at = pl.ds(pl.multiple_of(xx * NY + c * 128, 128), 128)
                total = accs[0][at, :]
                for acc in accs[1:]:
                    total = total + acc[at, :]
                back = total.T
                for q in range(GROUPS):
                    to = pl.ds(xx + XG * q, LEV, stride=CX)
                    xs[c, to, :] = xs[c, to, :] + back[q * LEV : (q + 1) * LEV]

        stores[c].start()
    for copy in stores:
        copy.wait()


def scatter(rows, packed, dual, quarter, weights):
    return pl.pallas_call(
        scatter_kernel,
        out_shape=jax.ShapeDtypeStruct((LEV * CX, NY), F32),
        in_specs=[vmem_spec(), vmem_spec(), any_spec(), vmem_spec(), vmem_spec()],
        out_specs=any_spec(),
        scratch_shapes=[
            pltpu.VMEM((4, LEV * CX, 128), F32),
            pltpu.VMEM((TAPS * OB, 128), F32),
            pltpu.VMEM((TAPS * OB, 128), F32),
            pltpu.SemaphoreType.DMA((4,)),
            pltpu.SemaphoreType.DMA((RING,)),
        ]
        + [pltpu.SMEM((TAPS, OB), jnp.int32)] * RING
        + [pltpu.VMEM((TROWS, 128), F32)] * NACC,
        compiler_params=pltpu.CompilerParams(vmem_limit_bytes=46 << 20),
        cost_estimate=pl.CostEstimate(flops=40_000_000, bytes_accessed=120_000_000, transcendentals=0),
        name="spread",
    )(rows, packed, dual, quarter, weights)


def split(a):
    high = a.astype(BF16)
    return high, (a - high.astype(F32)).astype(BF16)


DOT = functools.partial(lax.dot_general, preferred_element_type=F32)
PLAIN, BY_ROWS = (((1,), (0,)), ((), ())), (((1,), (1,)), ((), ()))
WIDE = LEV * SUBL
BLOCKS = CX // SUBL


def widen(mix_ref, wide, transposed):
    row = lax.broadcasted_iota(jnp.int32, (WIDE, LEV), 0)
    col = lax.broadcasted_iota(jnp.int32, (WIDE, LEV), 1)
    spread = jnp.where(row // SUBL == col, 1.0, 0.0).astype(BF16)
    rows = lax.broadcasted_iota(jnp.int32, (WIDE, WIDE), 0)
    cols = lax.broadcasted_iota(jnp.int32, (WIDE, WIDE), 1)
    same = rows % SUBL == cols % SUBL
    for h, part in enumerate(split(mix_ref[0])):
        half = DOT(spread, part, BY_ROWS if transposed else PLAIN).astype(BF16)
        wide[h] = jnp.where(same, DOT(half, spread, BY_ROWS), 0.0).astype(BF16)


def laplace_at(ring, slots, level, row, col):
    before, cur, after = (ring[slot, level] for slot in slots)
    up = pltpu.roll(jnp.where(row == SUBL - 1, before, cur), 1, 0)
    down = pltpu.roll(jnp.where(row == 0, after, cur), SUBL - 1, 0)
    left = jnp.where(col == 0, 0.0, pltpu.roll(cur, 1, 1))
    right = jnp.where(col == NY - 1, 0.0, pltpu.roll(cur, NY - 1, 1))
    return (up + down) + (left + right) - 4.0 * cur


def rows_at(block):
    return pl.ds(pl.multiple_of(block * SUBL, SUBL), SUBL)


def copy_in(hbm, buf, sem, block):
    return pltpu.make_async_copy(hbm.at[0, :, rows_at(block), :], buf.at[block], sem.at[block])


def copy_out(buf, hbm, sem, block):
    return pltpu.make_async_copy(buf.at[block], hbm.at[0, :, rows_at(block), :], sem.at[block])


def stencil_steps(mix_ref, src, lo_ref, hi_ref, edge_at, scale, write, after, wait, ring, mixes, wide, transposed):
    widen(mix_ref, wide, transposed)
    for level in range(LEV):
        ring[2, level] = jnp.broadcast_to(lo_ref[edge_at + level], (SUBL, NY))

    @pl.loop(0, BLOCKS + 1)
    def _(step):
        now = lax.rem(step, 3)
        slots, old = (lax.rem(step + 1, 3), lax.rem(step + 2, 3), now), lax.rem(step + 1, 2)
        block, done = jnp.minimum(step, BLOCKS - 1), jnp.maximum(step - 1, 0)

        @pl.when(step < BLOCKS)
        def _():
            wait(step)

        for level in range(LEV):
            ring[now, level] = scale(src[block, level], block)

        @pl.when(step == BLOCKS)
        def _():
            for level in range(LEV):
                ring[now, level] = jnp.broadcast_to(hi_ref[edge_at + level], (SUBL, NY))

        row = lax.broadcasted_iota(jnp.int32, (SUBL, NY), 0)
        col = lax.broadcasted_iota(jnp.int32, (SUBL, NY), 1)
        for level in range(LEV):
            mix = mixes[old, level * SUBL : (level + 1) * SUBL, :]
            write(done, level, mix, laplace_at(ring, slots, level, row, col))
        high, low = split(src[block].reshape(WIDE, NY))
        mh, ml = wide[0], wide[1]
        mixes[1 - old] = DOT(mh, high, PLAIN) + (DOT(mh, low, PLAIN) + DOT(ml, high, PLAIN))

        @pl.when(step > 0)
        def _():
            after(step - 1)


def adjoint_kernel(mix_ref, d_hbm, lo_ref, hi_ref, diff_ref, o_hbm, src, out, in_sem, out_sem, ring, mixes, wide):
    @pl.loop(0, BLOCKS)
    def _(block):
        copy_in(d_hbm, src, in_sem, block).start()

    def scale(field, block):
        return field * diff_ref[0, rows_at(block), :]

    def write(block, level, mix, lap):
        out[block, level] = mix + lap

    def wait(block):
        copy_in(d_hbm, src, in_sem, block).wait()

    def after(block):
        copy_out(out, o_hbm, out_sem, block).start()

    stencil_steps(mix_ref, src, lo_ref, hi_ref, LEV, scale, write, after, wait, ring, mixes, wide, True)

    @pl.loop(0, BLOCKS)
    def _(block):
        copy_out(out, o_hbm, out_sem, block).wait()


def final_kernel(
    mix_ref,
    p_hbm,
    back_hbm,
    lo_ref,
    hi_ref,
    diff_ref,
    base_ref,
    obs_ref,
    o_hbm,
    s_hbm,
    src,
    out,
    in_sem,
    out_sem,
    ring,
    mixes,
    wide,
    back,
    state,
    back_sem,
    state_sem,
):
    @pl.loop(0, BLOCKS)
    def _(block):
        copy_in(p_hbm, src, in_sem, block).start()
        copy_in(back_hbm, back, back_sem, block).start()

    def write(block, level, mix, lap):
        at = rows_at(block)
        out[block, level] = base_ref[0, level, at, :] - (mix + diff_ref[0, at, :] * lap)

    def wait(block):
        copy_in(p_hbm, src, in_sem, block).wait()

    def after(block):
        copy_out(out, o_hbm, out_sem, block).start()
        copy_in(back_hbm, back, back_sem, block).wait()
        for level in range(LEV):
            state[block, level] = obs_ref[0, level, rows_at(block), :] - back[block, level]
        copy_out(state, s_hbm, state_sem, block).start()

    stencil_steps(
        mix_ref, src, lo_ref, hi_ref, 0, lambda field, block: field, write, after, wait, ring, mixes, wide, False
    )

    @pl.loop(0, BLOCKS)
    def _(block):
        copy_out(out, o_hbm, out_sem, block).wait()
        copy_out(state, s_hbm, state_sem, block).wait()


FIELD = jax.ShapeDtypeStruct((1, LEV, CX, NY), F32)
STENCIL_SCRATCH = [
    pltpu.VMEM((BLOCKS, LEV, SUBL, NY), F32),
    pltpu.VMEM((BLOCKS, LEV, SUBL, NY), F32),
    pltpu.SemaphoreType.DMA((BLOCKS,)),
    pltpu.SemaphoreType.DMA((BLOCKS,)),
    pltpu.VMEM((3, LEV, SUBL, NY), F32),
    pltpu.VMEM((2, WIDE, NY), F32),
    pltpu.VMEM((2, WIDE, WIDE), BF16),
]


def final_of(mix, prior, back, lo, hi, diff, base, with_obs):
    return pl.pallas_call(
        final_kernel,
        out_shape=[FIELD, FIELD],
        in_specs=[vmem_spec(), any_spec(), any_spec()] + [vmem_spec()] * 5,
        out_specs=[any_spec(), any_spec()],
        scratch_shapes=STENCIL_SCRATCH
        + [pltpu.VMEM((BLOCKS, LEV, SUBL, NY), F32)] * 2
        + [pltpu.SemaphoreType.DMA((BLOCKS,))] * 2,
        compiler_params=pltpu.CompilerParams(vmem_limit_bytes=30 << 20),
        cost_estimate=pl.CostEstimate(flops=2_000_000_000, bytes_accessed=24_000_000, transcendentals=0),
        name="final",
    )(mix, prior, back, lo, hi, diff, base, with_obs)


def adjoint_of(mix, dual, lo, hi, diff):
    return pl.pallas_call(
        adjoint_kernel,
        out_shape=FIELD,
        in_specs=[vmem_spec(), any_spec(), vmem_spec(), vmem_spec(), vmem_spec()],
        out_specs=any_spec(),
        scratch_shapes=STENCIL_SCRATCH,
        compiler_params=pltpu.CompilerParams(vmem_limit_bytes=VMEM_LIMIT),
        cost_estimate=pl.CostEstimate(flops=2_000_000_000, bytes_accessed=12_000_000, transcendentals=0),
        name="adjoint",
    )(mix, dual, lo, hi, diff)


def whole_spec(shape):
    return pl.BlockSpec(shape, lambda g: (0,) * len(shape))


BLOCK, DIFF = ((1, LEV, SUBL, NY), 2), ((1, SUBL, NY), 1)
EDGES = (2 * LEV, 1, NY)


def place(tile_ref, count, step):
    for tile in range(16):
        count[tile] = 0

    @pl.loop(0, NBLOCK)
    def _(j):
        tile = tile_ref[j]
        slot = count[tile]
        count[tile] = slot + 1
        step(j, tile * MOST + slot)


def prepare_kernel(
    tile_ref, d_ref, x0_ref, x7_ref, m0_ref, m7_ref, f0_ref, f7_ref, o_ref, first_ref, last_ref, count
):
    for level in range(LEV):
        first_ref[level] = x0_ref[0, level, 0:1, :]
        last_ref[level] = x7_ref[0, level, SUBL - 1 : SUBL, :]
        first_ref[LEV + level] = m0_ref[0, level, 0:1, :] * f0_ref[0, 0:1, :]
        last_ref[LEV + level] = m7_ref[0, level, SUBL - 1 : SUBL, :] * f7_ref[0, SUBL - 1 : SUBL, :]
    o_ref[...] = jnp.zeros((SLOTS, LEV, OB), F32)

    def step(j, at):
        o_ref[at] = d_ref[j]

    place(tile_ref, count, step)


def prepare(tile, blocks, x, dual, diff):
    def at(place, shape, dim):
        return pl.BlockSpec(shape, lambda g: tuple(place if d == dim else 0 for d in range(len(shape))))

    end = BLOCKS - 1
    return pl.pallas_call(
        prepare_kernel,
        out_shape=[jax.ShapeDtypeStruct((SLOTS, LEV, OB), F32)] + [jax.ShapeDtypeStruct(EDGES, F32)] * 2,
        grid=(1,),
        in_specs=[
            pl.BlockSpec(memory_space=pltpu.SMEM),
            whole_spec((NBLOCK, LEV, OB)),
            at(0, *BLOCK),
            at(end, *BLOCK),
            at(0, *BLOCK),
            at(end, *BLOCK),
            at(0, *DIFF),
            at(end, *DIFF),
        ],
        out_specs=[whole_spec((SLOTS, LEV, OB)), whole_spec(EDGES), whole_spec(EDGES)],
        scratch_shapes=[pltpu.SMEM((16,), jnp.int32)],
        compiler_params=pltpu.CompilerParams(vmem_limit_bytes=VMEM_LIMIT),
        cost_estimate=pl.CostEstimate(flops=1_000_000, bytes_accessed=4_000_000, transcendentals=0),
        name="prepare",
    )(tile, blocks, x, x, dual, dual, diff, diff)


def unpack_kernel(tile_ref, got_ref, var_ref, d_ref, o_ref, count):
    def step(j, at):
        o_ref[j] = var_ref[j] * d_ref[j] + got_ref[at]

    place(tile_ref, count, step)


def unpack(tile, got, var, blocks):
    return pl.pallas_call(
        unpack_kernel,
        out_shape=jax.ShapeDtypeStruct((NBLOCK, LEV, OB), F32),
        in_specs=[pl.BlockSpec(memory_space=pltpu.SMEM)] + [vmem_spec()] * 3,
        out_specs=vmem_spec(),
        scratch_shapes=[pltpu.SMEM((16,), jnp.int32)],
        compiler_params=pltpu.CompilerParams(vmem_limit_bytes=8 << 20),
        cost_estimate=pl.CostEstimate(flops=1_000_000, bytes_accessed=3_000_000, transcendentals=0),
        name="unpack",
    )(tile, got, var, blocks)


def moved(block, dtm, dspace):
    ntm, nspace = lax.axis_size("tm"), lax.axis_size("space")
    pairs = [
        (t * nspace + s, ((t + dtm) % ntm) * nspace + s + dspace)
        for t in range(ntm)
        for s in range(nspace)
        if 0 <= s + dspace < nspace
    ]
    return lax.ppermute(block, ("tm", "space"), pairs)


def on_device(
    dual_model,
    state_incr,
    dual_obs,
    model_var,
    obs_var,
    level_mix,
    diffusivity,
    obs_tile,
    obs_cells,
    obs_weights,
):
    tile = obs_tile.reshape(NBLOCK)
    packed, first, last = prepare(tile, dual_obs[0], state_incr, dual_model, diffusivity)
    lo, hi = moved(last, 0, 1), moved(first, 0, -1)
    packed, lo, hi = lax.optimization_barrier((packed, lo, hi))
    got_dual = lax.all_to_all(packed, "space", split_axis=0, concat_axis=0, tiled=True)
    halo = moved(jnp.concatenate([lo[:LEV], hi[:LEV]]), 1, 0)

    adjoint = adjoint_of(level_mix, dual_model, lo, hi, diffusivity)
    sent, adjoint, got_dual, halo, field = lax.optimization_barrier(
        (state_incr, adjoint, got_dual, halo, state_incr)
    )
    prior = moved(sent, 1, 0)
    back = moved(adjoint, -1, 0)

    cells = obs_cells.reshape(SLOTS, TAPS, OB)
    weights = obs_weights.reshape(SLOTS, TAPS, OB)
    rows, quarter = cells & (TROWS - 1), lax.shift_right_logical(cells, 13)
    interp = gather(rows, field.reshape(LEV * CX, NY), quarter, weights)
    interp, got_dual = lax.optimization_barrier((interp, got_dual))
    got_interp = lax.all_to_all(interp, "space", split_axis=0, concat_axis=0, tiled=True)
    with_obs = scatter(rows, got_dual, dual_model.reshape(LEV * CX, NY), quarter, weights)

    with_obs, var = lax.optimization_barrier((with_obs, model_var))
    base = var * dual_model + state_incr
    base, with_obs = lax.optimization_barrier((base, with_obs))
    model_rows, state_rows = final_of(
        level_mix, prior, back, halo[:LEV], halo[LEV:], diffusivity, base, with_obs.reshape(1, LEV, CX, NY)
    )
    state_rows, var_obs = lax.optimization_barrier((state_rows, obs_var))
    obs_rows = unpack(tile, got_interp, var_obs[0], dual_obs[0])
    return (model_rows, obs_rows[None], state_rows)


def solution(mesh):
    field = P("tm", None, "space", None)
    blocks = P("tm", "space", None, None)
    taps = P("tm", "space", None, None, None, None)
    placed = (
        field,
        field,
        blocks,
        field,
        blocks,
        P("tm", None, None),
        P("tm", "space", None),
        P("tm", "space", None),
        taps,
        taps,
    )
    return jax.shard_map(
        on_device,
        mesh=mesh,
        in_specs=placed,
        out_specs=(field, blocks, field),
        check_vma=False,
    )
```

```python
import functools

import jax
import jax.numpy as jnp
from jax import lax
from jax.experimental import pallas as pl
from jax.experimental.pallas import tpu as pltpu
from jax.sharding import PartitionSpec as P

HIGH = lax.Precision.HIGHEST
F32 = jnp.float32
BF16 = jnp.bfloat16

LEV, CX, NY = 32, 64, 512
SLOTS, TAPS, OB = 64, 4, 128
NBLOCK, MOST = 24, 4
GROUPS = 4
TROWS = CX * NY // GROUPS
XG = CX // GROUPS
SUBL = 8
NACC = 8
VMEM_LIMIT = 60 << 20
RING = 4


def any_spec():
    return pl.BlockSpec(memory_space=pl.ANY)


def vmem_spec():
    return pl.BlockSpec(memory_space=pltpu.VMEM)


def gather_kernel(rows_ref, x_hbm, q_ref, w_ref, o_ref, xs, tab, raw0, raw1, xsem, isem, *idxs):
    raws = (raw0, raw1)

    def fetch(s, par):
        return pltpu.make_async_copy(rows_ref.at[s], idxs[par], isem.at[par])

    copies = [
        pltpu.make_async_copy(x_hbm.at[:, pl.ds(c * 128, 128)], xs.at[c], xsem.at[c])
        for c in range(4)
    ]
    for copy in copies:
        copy.start()
    for r in range(RING):
        fetch(r, r).start()
    for c in range(4):
        copies[c].wait()

        @pl.loop(0, XG // 4)
        def _(x4):
            for i in range(4):
                xx = x4 * 4 + i
                block = jnp.concatenate(
                    [xs[c, pl.ds(xx + XG * q, LEV, stride=CX), :] for q in range(GROUPS)], axis=0
                )
                tab[pl.ds(pl.multiple_of(xx * NY + c * 128, 128), 128), :] = block.T

    def finish(s, raw):
        w4, q4 = w_ref[s], q_ref[s]
        total = jnp.zeros((LEV, OB), F32)
        for t in range(TAPS):
            a = raw[t * OB : (t + 1) * OB, :].T
            for q in range(GROUPS):
                total = total + a[q * LEV : (q + 1) * LEV] * jnp.where(
                    q4[t : t + 1] == q, w4[t : t + 1], 0.0
                )
        o_ref[s] = total

    @pl.loop(0, SLOTS // RING)
    def _(group):
        for r in range(RING):
            s, par = group * RING + r, r % 2
            fetch(s, r).wait()
            finish(jnp.maximum(s - 1, 0), raws[1 - par])
            for t in range(TAPS):
                for b in range(OB):
                    i = idxs[r][t, b]
                    raws[par][t * OB + b : t * OB + b + 1, :] = tab[pl.ds(i, 1), :]

            @pl.when(s + RING < SLOTS)
            def _():
                fetch(s + RING, r).start()

    finish(SLOTS - 1, raws[1])


def gather(rows, field, quarter, weights):
    return pl.pallas_call(
        gather_kernel,
        out_shape=jax.ShapeDtypeStruct((SLOTS, LEV, OB), F32),
        in_specs=[vmem_spec(), any_spec(), vmem_spec(), vmem_spec()],
        out_specs=vmem_spec(),
        scratch_shapes=[
            pltpu.VMEM((4, LEV * CX, 128), F32),
            pltpu.VMEM((TROWS, 128), F32),
            pltpu.VMEM((TAPS * OB, 128), F32),
            pltpu.VMEM((TAPS * OB, 128), F32),
            pltpu.SemaphoreType.DMA((4,)),
            pltpu.SemaphoreType.DMA((RING,)),
        ]
        + [pltpu.SMEM((TAPS, OB), jnp.int32)] * RING,
        compiler_params=pltpu.CompilerParams(vmem_limit_bytes=VMEM_LIMIT),
        cost_estimate=pl.CostEstimate(flops=40_000_000, bytes_accessed=100_000_000, transcendentals=0),
        name="interpolate",
    )(rows, field, quarter, weights)


def scatter_kernel(rows_ref, d_ref, dual_hbm, q_ref, w_ref, o_hbm, xs, prod0, prod1, xsem, isem, *rest):
    prods, idxs, accs = (prod0, prod1), rest[:RING], rest[RING:]

    def fetch(s, par):
        return pltpu.make_async_copy(rows_ref.at[s], idxs[par], isem.at[par])

    loads = [
        pltpu.make_async_copy(dual_hbm.at[:, pl.ds(c * 128, 128)], xs.at[c], xsem.at[c])
        for c in range(4)
    ]
    for copy in loads:
        copy.start()
    for r in range(RING):
        fetch(r, r).start()
    zero = jnp.zeros((64, 128), F32)

    @pl.loop(0, TROWS // 64)
    def _(i):
        for acc in accs:
            acc[pl.ds(pl.multiple_of(i * 64, 64), 64), :] = zero

    def prepare(s, prod):
        w4, q4, d = w_ref[s], q_ref[s], d_ref[s]
        for t in range(TAPS):
            a = jnp.concatenate(
                [d * jnp.where(q4[t : t + 1] == q, w4[t : t + 1], 0.0) for q in range(GROUPS)],
                axis=0,
            )
            prod[t * OB : (t + 1) * OB, :] = a.T

    prepare(0, prods[0])
    per = NACC // TAPS

    @pl.loop(0, SLOTS // RING)
    def _(group):
        for r in range(RING):
            s, par = group * RING + r, r % 2
            fetch(s, r).wait()
            prepare(jnp.minimum(s + 1, SLOTS - 1), prods[1 - par])
            for g in range(OB // per):
                news = []
                for j in range(per):
                    for t in range(TAPS):
                        b = g * per + j
                        i = idxs[r][t, b]
                        new = accs[j * TAPS + t][pl.ds(i, 1), :] + prods[par][t * OB + b : t * OB + b + 1, :]
                        news.append((i, new))
                for k, (i, new) in enumerate(news):
                    accs[k][pl.ds(i, 1), :] = new

            @pl.when(s + RING < SLOTS)
            def _():
                fetch(s + RING, r).start()

    stores = [
        pltpu.make_async_copy(xs.at[c], o_hbm.at[:, pl.ds(c * 128, 128)], xsem.at[c])
        for c in range(4)
    ]
    for c in range(4):
        loads[c].wait()

        @pl.loop(0, XG // 4)
        def _(x4):
            for i in range(4):
                xx = x4 * 4 + i
                at = pl.ds(pl.multiple_of(xx * NY + c * 128, 128), 128)
                total = accs[0][at, :]
                for acc in accs[1:]:
                    total = total + acc[at, :]
                back = total.T
                for q in range(GROUPS):
                    to = pl.ds(xx + XG * q, LEV, stride=CX)
                    xs[c, to, :] = xs[c, to, :] + back[q * LEV : (q + 1) * LEV]

        stores[c].start()
    for copy in stores:
        copy.wait()


def scatter(rows, packed, dual, quarter, weights):
    return pl.pallas_call(
        scatter_kernel,
        out_shape=jax.ShapeDtypeStruct((LEV * CX, NY), F32),
        in_specs=[vmem_spec(), vmem_spec(), any_spec(), vmem_spec(), vmem_spec()],
        out_specs=any_spec(),
        scratch_shapes=[
            pltpu.VMEM((4, LEV * CX, 128), F32),
            pltpu.VMEM((TAPS * OB, 128), F32),
            pltpu.VMEM((TAPS * OB, 128), F32),
            pltpu.SemaphoreType.DMA((4,)),
            pltpu.SemaphoreType.DMA((RING,)),
        ]
        + [pltpu.SMEM((TAPS, OB), jnp.int32)] * RING
        + [pltpu.VMEM((TROWS, 128), F32)] * NACC,
        compiler_params=pltpu.CompilerParams(vmem_limit_bytes=46 << 20),
        cost_estimate=pl.CostEstimate(flops=40_000_000, bytes_accessed=120_000_000, transcendentals=0),
        name="spread",
    )(rows, packed, dual, quarter, weights)


def split(a):
    high = a.astype(BF16)
    return high, (a - high.astype(F32)).astype(BF16)


DOT = functools.partial(lax.dot_general, preferred_element_type=F32)
PLAIN, BY_ROWS = (((1,), (0,)), ((), ())), (((1,), (1,)), ((), ()))
WIDE = LEV * SUBL
BLOCKS = CX // SUBL


def widen(mix_ref, wide, transposed):
    row = lax.broadcasted_iota(jnp.int32, (WIDE, LEV), 0)
    col = lax.broadcasted_iota(jnp.int32, (WIDE, LEV), 1)
    spread = jnp.where(row // SUBL == col, 1.0, 0.0).astype(BF16)
    rows = lax.broadcasted_iota(jnp.int32, (WIDE, WIDE), 0)
    cols = lax.broadcasted_iota(jnp.int32, (WIDE, WIDE), 1)
    same = rows % SUBL == cols % SUBL
    for h, part in enumerate(split(mix_ref[0])):
        half = DOT(spread, part, BY_ROWS if transposed else PLAIN).astype(BF16)
        wide[h] = jnp.where(same, DOT(half, spread, BY_ROWS), 0.0).astype(BF16)


def laplace_at(ring, slots, level, row, col):
    before, cur, after = (ring[slot, level] for slot in slots)
    up = pltpu.roll(jnp.where(row == SUBL - 1, before, cur), 1, 0)
    down = pltpu.roll(jnp.where(row == 0, after, cur), SUBL - 1, 0)
    left = jnp.where(col == 0, 0.0, pltpu.roll(cur, 1, 1))
    right = jnp.where(col == NY - 1, 0.0, pltpu.roll(cur, NY - 1, 1))
    return (up + down) + (left + right) - 4.0 * cur


def rows_at(block):
    return pl.ds(pl.multiple_of(block * SUBL, SUBL), SUBL)


def copy_in(hbm, buf, sem, block):
    return pltpu.make_async_copy(hbm.at[0, :, rows_at(block), :], buf.at[block], sem.at[block])


def copy_out(buf, hbm, sem, block):
    return pltpu.make_async_copy(buf.at[block], hbm.at[0, :, rows_at(block), :], sem.at[block])


def edge_block(edge_ref, level):
    if edge_ref is None:
        return jnp.zeros((SUBL, NY), F32)
    return jnp.broadcast_to(edge_ref[level], (SUBL, NY))


def stencil_steps(mix_ref, src, lo_ref, hi_ref, scale, write, after, wait, ring, mixes, wide, transposed):
    widen(mix_ref, wide, transposed)
    for level in range(LEV):
        ring[2, level] = edge_block(lo_ref, level)

    @pl.loop(0, BLOCKS + 1)
    def _(step):
        now = lax.rem(step, 3)
        slots, old = (lax.rem(step + 1, 3), lax.rem(step + 2, 3), now), lax.rem(step + 1, 2)
        block, done = jnp.minimum(step, BLOCKS - 1), jnp.maximum(step - 1, 0)

        @pl.when(step < BLOCKS)
        def _():
            wait(step)

        for level in range(LEV):
            ring[now, level] = scale(src[block, level], block)

        @pl.when(step == BLOCKS)
        def _():
            for level in range(LEV):
                ring[now, level] = edge_block(hi_ref, level)

        row = lax.broadcasted_iota(jnp.int32, (SUBL, NY), 0)
        col = lax.broadcasted_iota(jnp.int32, (SUBL, NY), 1)
        for level in range(LEV):
            mix = mixes[old, level * SUBL : (level + 1) * SUBL, :]
            write(done, level, mix, laplace_at(ring, slots, level, row, col))
        high, low = split(src[block].reshape(WIDE, NY))
        mh, ml = wide[0], wide[1]
        mixes[1 - old] = DOT(mh, high, PLAIN) + (DOT(mh, low, PLAIN) + DOT(ml, high, PLAIN))

        @pl.when(step > 0)
        def _():
            after(step - 1)


def adjoint_kernel(mix_ref, d_hbm, diff_ref, o_hbm, src, out, in_sem, out_sem, ring, mixes, wide):
    @pl.loop(0, BLOCKS)
    def _(block):
        copy_in(d_hbm, src, in_sem, block).start()

    def scale(field, block):
        return field * diff_ref[0, rows_at(block), :]

    def write(block, level, mix, lap):
        out[block, level] = mix + lap

    def wait(block):
        copy_in(d_hbm, src, in_sem, block).wait()

    def after(block):
        copy_out(out, o_hbm, out_sem, block).start()

    stencil_steps(mix_ref, src, None, None, scale, write, after, wait, ring, mixes, wide, True)

    @pl.loop(0, BLOCKS)
    def _(block):
        copy_out(out, o_hbm, out_sem, block).wait()


def final_kernel(
    mix_ref,
    p_hbm,
    back_hbm,
    halo_ref,
    edge_ref,
    diff_ref,
    base_ref,
    obs_ref,
    o_hbm,
    s_hbm,
    src,
    out,
    in_sem,
    out_sem,
    ring,
    mixes,
    wide,
    back,
    state,
    back_sem,
    state_sem,
):
    @pl.loop(0, BLOCKS)
    def _(block):
        copy_in(p_hbm, src, in_sem, block).start()
        copy_in(back_hbm, back, back_sem, block).start()

    def write(block, level, mix, lap):
        at = rows_at(block)
        out[block, level] = base_ref[0, level, at, :] - (mix + diff_ref[0, at, :] * lap)

    def wait(block):
        copy_in(p_hbm, src, in_sem, block).wait()

    def after(block):
        copy_out(out, o_hbm, out_sem, block).start()
        copy_in(back_hbm, back, back_sem, block).wait()
        for level in range(LEV):
            state[block, level] = obs_ref[0, level, rows_at(block), :] - back[block, level]

        @pl.when(block == 0)
        def _():
            for level in range(LEV):
                state[0, level, 0:1, :] = state[0, level, 0:1, :] - edge_ref[level]

        @pl.when(block == BLOCKS - 1)
        def _():
            for level in range(LEV):
                at = SUBL - 1
                state[BLOCKS - 1, level, at:, :] = state[BLOCKS - 1, level, at:, :] - edge_ref[LEV + level]

        copy_out(state, s_hbm, state_sem, block).start()

    lo_ref, hi_ref = halo_ref.at[pl.ds(0, LEV)], halo_ref.at[pl.ds(LEV, LEV)]
    stencil_steps(
        mix_ref, src, lo_ref, hi_ref, lambda field, block: field, write, after, wait, ring, mixes, wide, False
    )

    @pl.loop(0, BLOCKS)
    def _(block):
        copy_out(out, o_hbm, out_sem, block).wait()
        copy_out(state, s_hbm, state_sem, block).wait()


FIELD = jax.ShapeDtypeStruct((1, LEV, CX, NY), F32)
STENCIL_SCRATCH = [
    pltpu.VMEM((BLOCKS, LEV, SUBL, NY), F32),
    pltpu.VMEM((BLOCKS, LEV, SUBL, NY), F32),
    pltpu.SemaphoreType.DMA((BLOCKS,)),
    pltpu.SemaphoreType.DMA((BLOCKS,)),
    pltpu.VMEM((3, LEV, SUBL, NY), F32),
    pltpu.VMEM((2, WIDE, NY), F32),
    pltpu.VMEM((2, WIDE, WIDE), BF16),
]


def final_of(mix, prior, back, halo, edges, diff, base, with_obs):
    return pl.pallas_call(
        final_kernel,
        out_shape=[FIELD, FIELD],
        in_specs=[vmem_spec(), any_spec(), any_spec()] + [vmem_spec()] * 5,
        out_specs=[any_spec(), any_spec()],
        scratch_shapes=STENCIL_SCRATCH
        + [pltpu.VMEM((BLOCKS, LEV, SUBL, NY), F32)] * 2
        + [pltpu.SemaphoreType.DMA((BLOCKS,))] * 2,
        compiler_params=pltpu.CompilerParams(vmem_limit_bytes=30 << 20),
        cost_estimate=pl.CostEstimate(flops=2_000_000_000, bytes_accessed=24_000_000, transcendentals=0),
        name="final",
    )(mix, prior, back, halo, edges, diff, base, with_obs)


def adjoint_of(mix, dual, diff):
    return pl.pallas_call(
        adjoint_kernel,
        out_shape=FIELD,
        in_specs=[vmem_spec(), any_spec(), vmem_spec()],
        out_specs=any_spec(),
        scratch_shapes=STENCIL_SCRATCH,
        compiler_params=pltpu.CompilerParams(vmem_limit_bytes=VMEM_LIMIT),
        cost_estimate=pl.CostEstimate(flops=2_000_000_000, bytes_accessed=12_000_000, transcendentals=0),
        name="adjoint",
    )(mix, dual, diff)


def whole_spec(shape):
    return pl.BlockSpec(shape, lambda g: (0,) * len(shape))


BLOCK, DIFF = ((1, LEV, SUBL, NY), 2), ((1, SUBL, NY), 1)
EDGES = (2 * LEV, 1, NY)


def place(tile_ref, count, step):
    for tile in range(16):
        count[tile] = 0

    @pl.loop(0, NBLOCK)
    def _(j):
        tile = tile_ref[j]
        slot = count[tile]
        count[tile] = slot + 1
        step(j, tile * MOST + slot)


def prepare_kernel(
    tile_ref, d_ref, x0_ref, x7_ref, m0_ref, m7_ref, f0_ref, f7_ref, o_ref, first_ref, last_ref, count
):
    for level in range(LEV):
        first_ref[level] = x0_ref[0, level, 0:1, :]
        last_ref[level] = x7_ref[0, level, SUBL - 1 : SUBL, :]
        first_ref[LEV + level] = m0_ref[0, level, 0:1, :] * f0_ref[0, 0:1, :]
        last_ref[LEV + level] = m7_ref[0, level, SUBL - 1 : SUBL, :] * f7_ref[0, SUBL - 1 : SUBL, :]
    o_ref[...] = jnp.zeros((SLOTS, LEV, OB), F32)

    def step(j, at):
        o_ref[at] = d_ref[j]

    place(tile_ref, count, step)


def prepare(tile, blocks, x, dual, diff):
    def at(place, shape, dim):
        return pl.BlockSpec(shape, lambda g: tuple(place if d == dim else 0 for d in range(len(shape))))

    end = BLOCKS - 1
    return pl.pallas_call(
        prepare_kernel,
        out_shape=[jax.ShapeDtypeStruct((SLOTS, LEV, OB), F32)] + [jax.ShapeDtypeStruct(EDGES, F32)] * 2,
        grid=(1,),
        in_specs=[
            pl.BlockSpec(memory_space=pltpu.SMEM),
            whole_spec((NBLOCK, LEV, OB)),
            at(0, *BLOCK),
            at(end, *BLOCK),
            at(0, *BLOCK),
            at(end, *BLOCK),
            at(0, *DIFF),
            at(end, *DIFF),
        ],
        out_specs=[whole_spec((SLOTS, LEV, OB)), whole_spec(EDGES), whole_spec(EDGES)],
        scratch_shapes=[pltpu.SMEM((16,), jnp.int32)],
        compiler_params=pltpu.CompilerParams(vmem_limit_bytes=VMEM_LIMIT),
        cost_estimate=pl.CostEstimate(flops=1_000_000, bytes_accessed=4_000_000, transcendentals=0),
        name="prepare",
    )(tile, blocks, x, x, dual, dual, diff, diff)


def unpack_kernel(tile_ref, got_ref, var_ref, d_ref, o_ref, count):
    def step(j, at):
        o_ref[j] = var_ref[j] * d_ref[j] + got_ref[at]

    place(tile_ref, count, step)


def unpack(tile, got, var, blocks):
    return pl.pallas_call(
        unpack_kernel,
        out_shape=jax.ShapeDtypeStruct((NBLOCK, LEV, OB), F32),
        in_specs=[pl.BlockSpec(memory_space=pltpu.SMEM)] + [vmem_spec()] * 3,
        out_specs=vmem_spec(),
        scratch_shapes=[pltpu.SMEM((16,), jnp.int32)],
        compiler_params=pltpu.CompilerParams(vmem_limit_bytes=8 << 20),
        cost_estimate=pl.CostEstimate(flops=1_000_000, bytes_accessed=3_000_000, transcendentals=0),
        name="unpack",
    )(tile, got, var, blocks)


def moved(block, dtm, dspace):
    ntm, nspace = lax.axis_size("tm"), lax.axis_size("space")
    pairs = [
        (t * nspace + s, ((t + dtm) % ntm) * nspace + s + dspace)
        for t in range(ntm)
        for s in range(nspace)
        if 0 <= s + dspace < nspace
    ]
    return lax.ppermute(block, ("tm", "space"), pairs)


def on_device(
    dual_model,
    state_incr,
    dual_obs,
    model_var,
    obs_var,
    level_mix,
    diffusivity,
    obs_tile,
    obs_cells,
    obs_weights,
):
    tile = obs_tile.reshape(NBLOCK)
    packed, first, last = prepare(tile, dual_obs[0], state_incr, dual_model, diffusivity)
    lo, hi = moved(last, 0, 1), moved(first, 0, -1)
    got_dual = lax.all_to_all(packed, "space", split_axis=0, concat_axis=0, tiled=True)

    diff, packed = lax.optimization_barrier((diffusivity, packed))
    adjoint = adjoint_of(level_mix, dual_model, diff)
    sent, adjoint, got_dual, lo, hi, field = lax.optimization_barrier(
        (state_incr, adjoint, got_dual, lo, hi, state_incr)
    )
    prior = moved(sent, 1, 0)
    back = moved(adjoint, -1, 0)
    halo = moved(jnp.concatenate([lo[:LEV], hi[:LEV]]), 1, 0)
    edges = moved(jnp.concatenate([lo[LEV:], hi[LEV:]]), -1, 0)

    cells = obs_cells.reshape(SLOTS, TAPS, OB)
    weights = obs_weights.reshape(SLOTS, TAPS, OB)
    rows, quarter = cells & (TROWS - 1), lax.shift_right_logical(cells, 13)
    interp = gather(rows, field.reshape(LEV * CX, NY), quarter, weights)
    interp, got_dual = lax.optimization_barrier((interp, got_dual))
    got_interp = lax.all_to_all(interp, "space", split_axis=0, concat_axis=0, tiled=True)
    with_obs = scatter(rows, got_dual, dual_model.reshape(LEV * CX, NY), quarter, weights)

    with_obs, var = lax.optimization_barrier((with_obs, model_var))
    base = var * dual_model + state_incr
    base, with_obs = lax.optimization_barrier((base, with_obs))
    model_rows, state_rows = final_of(
        level_mix, prior, back, halo, edges, diffusivity, base, with_obs.reshape(1, LEV, CX, NY)
    )
    state_rows, var_obs = lax.optimization_barrier((state_rows, obs_var))
    obs_rows = unpack(tile, got_interp, var_obs[0], dual_obs[0])
    return (model_rows, obs_rows[None], state_rows)


def solution(mesh):
    field = P("tm", None, "space", None)
    blocks = P("tm", "space", None, None)
    taps = P("tm", "space", None, None, None, None)
    placed = (
        field,
        field,
        blocks,
        field,
        blocks,
        P("tm", None, None),
        P("tm", "space", None),
        P("tm", "space", None),
        taps,
        taps,
    )
    return jax.shard_map(
        on_device,
        mesh=mesh,
        in_specs=placed,
        out_specs=(field, blocks, field),
        check_vma=False,
    )
```

```python
import functools

import jax
import jax.numpy as jnp
from jax import lax
from jax.experimental import pallas as pl
from jax.experimental.pallas import tpu as pltpu
from jax.sharding import PartitionSpec as P

HIGH = lax.Precision.HIGHEST
F32 = jnp.float32
BF16 = jnp.bfloat16

LEV, CX, NY = 32, 64, 512
SLOTS, TAPS, OB = 64, 4, 128
NBLOCK, MOST = 24, 4
GROUPS = 4
TROWS = CX * NY // GROUPS
XG = CX // GROUPS
SUBL = 8
NACC = 8
VMEM_LIMIT = 60 << 20
RING = 4


def any_spec():
    return pl.BlockSpec(memory_space=pl.ANY)


def vmem_spec():
    return pl.BlockSpec(memory_space=pltpu.VMEM)


def gather_kernel(rows_ref, x_hbm, q_ref, w_ref, o_ref, xs, tab, raw0, raw1, xsem, isem, *idxs):
    raws = (raw0, raw1)

    def fetch(s, par):
        return pltpu.make_async_copy(rows_ref.at[s], idxs[par], isem.at[par])

    copies = [
        pltpu.make_async_copy(x_hbm.at[:, pl.ds(c * 128, 128)], xs.at[c], xsem.at[c])
        for c in range(4)
    ]
    for copy in copies:
        copy.start()
    for r in range(RING):
        fetch(r, r).start()
    for c in range(4):
        copies[c].wait()

        @pl.loop(0, XG // 4)
        def _(x4):
            for i in range(4):
                xx = x4 * 4 + i
                block = jnp.concatenate(
                    [xs[c, pl.ds(xx + XG * q, LEV, stride=CX), :] for q in range(GROUPS)], axis=0
                )
                tab[pl.ds(pl.multiple_of(xx * NY + c * 128, 128), 128), :] = block.T

    def finish(s, raw):
        w4, q4 = w_ref[s], q_ref[s]
        total = jnp.zeros((LEV, OB), F32)
        for t in range(TAPS):
            a = raw[t * OB : (t + 1) * OB, :].T
            for q in range(GROUPS):
                total = total + a[q * LEV : (q + 1) * LEV] * jnp.where(
                    q4[t : t + 1] == q, w4[t : t + 1], 0.0
                )
        o_ref[s] = total

    @pl.loop(0, SLOTS // RING)
    def _(group):
        for r in range(RING):
            s, par = group * RING + r, r % 2
            fetch(s, r).wait()
            finish(jnp.maximum(s - 1, 0), raws[1 - par])
            for t in range(TAPS):
                for b in range(OB):
                    i = idxs[r][t, b]
                    raws[par][t * OB + b : t * OB + b + 1, :] = tab[pl.ds(i, 1), :]

            @pl.when(s + RING < SLOTS)
            def _():
                fetch(s + RING, r).start()

    finish(SLOTS - 1, raws[1])


def gather(rows, field, quarter, weights):
    return pl.pallas_call(
        gather_kernel,
        out_shape=jax.ShapeDtypeStruct((SLOTS, LEV, OB), F32),
        in_specs=[vmem_spec(), any_spec(), vmem_spec(), vmem_spec()],
        out_specs=vmem_spec(),
        scratch_shapes=[
            pltpu.VMEM((4, LEV * CX, 128), F32),
            pltpu.VMEM((TROWS, 128), F32),
            pltpu.VMEM((TAPS * OB, 128), F32),
            pltpu.VMEM((TAPS * OB, 128), F32),
            pltpu.SemaphoreType.DMA((4,)),
            pltpu.SemaphoreType.DMA((RING,)),
        ]
        + [pltpu.SMEM((TAPS, OB), jnp.int32)] * RING,
        compiler_params=pltpu.CompilerParams(vmem_limit_bytes=VMEM_LIMIT),
        cost_estimate=pl.CostEstimate(flops=40_000_000, bytes_accessed=100_000_000, transcendentals=0),
        name="interpolate",
    )(rows, field, quarter, weights)


def scatter_kernel(rows_ref, d_ref, dual_hbm, q_ref, w_ref, o_hbm, xs, prod0, prod1, xsem, isem, *rest):
    prods, idxs, accs = (prod0, prod1), rest[:RING], rest[RING:]

    def fetch(s, par):
        return pltpu.make_async_copy(rows_ref.at[s], idxs[par], isem.at[par])

    loads = [
        pltpu.make_async_copy(dual_hbm.at[:, pl.ds(c * 128, 128)], xs.at[c], xsem.at[c])
        for c in range(4)
    ]
    for copy in loads:
        copy.start()
    for r in range(RING):
        fetch(r, r).start()
    zero = jnp.zeros((64, 128), F32)

    @pl.loop(0, TROWS // 64)
    def _(i):
        for acc in accs:
            acc[pl.ds(pl.multiple_of(i * 64, 64), 64), :] = zero

    def prepare(s, prod):
        w4, q4, d = w_ref[s], q_ref[s], d_ref[s]
        for t in range(TAPS):
            a = jnp.concatenate(
                [d * jnp.where(q4[t : t + 1] == q, w4[t : t + 1], 0.0) for q in range(GROUPS)],
                axis=0,
            )
            prod[t * OB : (t + 1) * OB, :] = a.T

    prepare(0, prods[0])
    per = NACC // TAPS

    @pl.loop(0, SLOTS // RING)
    def _(group):
        for r in range(RING):
            s, par = group * RING + r, r % 2
            fetch(s, r).wait()
            prepare(jnp.minimum(s + 1, SLOTS - 1), prods[1 - par])
            for g in range(OB // per):
                news = []
                for j in range(per):
                    for t in range(TAPS):
                        b = g * per + j
                        i = idxs[r][t, b]
                        new = accs[j * TAPS + t][pl.ds(i, 1), :] + prods[par][t * OB + b : t * OB + b + 1, :]
                        news.append((i, new))
                for k, (i, new) in enumerate(news):
                    accs[k][pl.ds(i, 1), :] = new

            @pl.when(s + RING < SLOTS)
            def _():
                fetch(s + RING, r).start()

    stores = [
        pltpu.make_async_copy(xs.at[c], o_hbm.at[:, pl.ds(c * 128, 128)], xsem.at[c])
        for c in range(4)
    ]
    for c in range(4):
        loads[c].wait()

        @pl.loop(0, XG // 4)
        def _(x4):
            for i in range(4):
                xx = x4 * 4 + i
                at = pl.ds(pl.multiple_of(xx * NY + c * 128, 128), 128)
                total = accs[0][at, :]
                for acc in accs[1:]:
                    total = total + acc[at, :]
                back = total.T
                for q in range(GROUPS):
                    to = pl.ds(xx + XG * q, LEV, stride=CX)
                    xs[c, to, :] = xs[c, to, :] + back[q * LEV : (q + 1) * LEV]

        stores[c].start()
    for copy in stores:
        copy.wait()


def scatter(rows, packed, dual, quarter, weights):
    return pl.pallas_call(
        scatter_kernel,
        out_shape=jax.ShapeDtypeStruct((LEV * CX, NY), F32),
        in_specs=[vmem_spec(), vmem_spec(), any_spec(), vmem_spec(), vmem_spec()],
        out_specs=any_spec(),
        scratch_shapes=[
            pltpu.VMEM((4, LEV * CX, 128), F32),
            pltpu.VMEM((TAPS * OB, 128), F32),
            pltpu.VMEM((TAPS * OB, 128), F32),
            pltpu.SemaphoreType.DMA((4,)),
            pltpu.SemaphoreType.DMA((RING,)),
        ]
        + [pltpu.SMEM((TAPS, OB), jnp.int32)] * RING
        + [pltpu.VMEM((TROWS, 128), F32)] * NACC,
        compiler_params=pltpu.CompilerParams(vmem_limit_bytes=46 << 20),
        cost_estimate=pl.CostEstimate(flops=40_000_000, bytes_accessed=120_000_000, transcendentals=0),
        name="spread",
    )(rows, packed, dual, quarter, weights)


def split(a):
    high = a.astype(BF16)
    return high, (a - high.astype(F32)).astype(BF16)


DOT = functools.partial(lax.dot_general, preferred_element_type=F32)
PLAIN, BY_ROWS = (((1,), (0,)), ((), ())), (((1,), (1,)), ((), ()))
WIDE = LEV * SUBL
BLOCKS = CX // SUBL


def widen(mix_ref, wide, transposed):
    row = lax.broadcasted_iota(jnp.int32, (WIDE, LEV), 0)
    col = lax.broadcasted_iota(jnp.int32, (WIDE, LEV), 1)
    spread = jnp.where(row // SUBL == col, 1.0, 0.0).astype(BF16)
    rows = lax.broadcasted_iota(jnp.int32, (WIDE, WIDE), 0)
    cols = lax.broadcasted_iota(jnp.int32, (WIDE, WIDE), 1)
    same = rows % SUBL == cols % SUBL
    for h, part in enumerate(split(mix_ref[0])):
        half = DOT(spread, part, BY_ROWS if transposed else PLAIN).astype(BF16)
        wide[h] = jnp.where(same, DOT(half, spread, BY_ROWS), 0.0).astype(BF16)


def laplace_at(ring, slots, level, row, col):
    before, cur, after = (ring[slot, level] for slot in slots)
    up = pltpu.roll(jnp.where(row == SUBL - 1, before, cur), 1, 0)
    down = pltpu.roll(jnp.where(row == 0, after, cur), SUBL - 1, 0)
    left = jnp.where(col == 0, 0.0, pltpu.roll(cur, 1, 1))
    right = jnp.where(col == NY - 1, 0.0, pltpu.roll(cur, NY - 1, 1))
    return (up + down) + (left + right) - 4.0 * cur


def rows_at(block):
    return pl.ds(pl.multiple_of(block * SUBL, SUBL), SUBL)


def copy_in(hbm, buf, sem, block):
    return pltpu.make_async_copy(hbm.at[0, :, rows_at(block), :], buf.at[block], sem.at[block])


def copy_out(buf, hbm, sem, block):
    return pltpu.make_async_copy(buf.at[block], hbm.at[0, :, rows_at(block), :], sem.at[block])


def edge_block(edge_ref, level):
    if edge_ref is None:
        return jnp.zeros((SUBL, NY), F32)
    return jnp.broadcast_to(edge_ref[level], (SUBL, NY))


def stencil_steps(mix_ref, src, lo_ref, hi_ref, scale, write, after, wait, ring, mixes, wide, transposed):
    widen(mix_ref, wide, transposed)
    for level in range(LEV):
        ring[2, level] = edge_block(lo_ref, level)

    def mix_block(to, block):
        high, low = split(src[block].reshape(WIDE, NY))
        mh, ml = wide[0], wide[1]
        mixes[to] = DOT(mh, high, PLAIN) + (DOT(mh, low, PLAIN) + DOT(ml, high, PLAIN))

    wait(0)
    for level in range(LEV):
        ring[0, level] = scale(src[0, level], 0)
    mix_block(0, 0)

    @pl.loop(1, BLOCKS + 1)
    def _(step):
        now = lax.rem(step, 3)
        slots, old = (lax.rem(step + 1, 3), lax.rem(step + 2, 3), now), lax.rem(step + 1, 2)
        block, done = jnp.minimum(step, BLOCKS - 1), step - 1

        @pl.when(step < BLOCKS)
        def _():
            wait(step)

        for level in range(LEV):
            ring[now, level] = scale(src[block, level], block)

        @pl.when(step == BLOCKS)
        def _():
            for level in range(LEV):
                ring[now, level] = edge_block(hi_ref, level)

        row = lax.broadcasted_iota(jnp.int32, (SUBL, NY), 0)
        col = lax.broadcasted_iota(jnp.int32, (SUBL, NY), 1)
        for level in range(LEV):
            mix = mixes[old, level * SUBL : (level + 1) * SUBL, :]
            write(done, level, mix, laplace_at(ring, slots, level, row, col))
        mix_block(1 - old, block)
        after(step - 1)


def adjoint_kernel(mix_ref, d_hbm, diff_ref, o_hbm, src, out, in_sem, out_sem, ring, mixes, wide):
    @pl.loop(0, BLOCKS)
    def _(block):
        copy_in(d_hbm, src, in_sem, block).start()

    def scale(field, block):
        return field * diff_ref[0, rows_at(block), :]

    def write(block, level, mix, lap):
        out[block, level] = mix + lap

    def wait(block):
        copy_in(d_hbm, src, in_sem, block).wait()

    def after(block):
        copy_out(out, o_hbm, out_sem, block).start()

    stencil_steps(mix_ref, src, None, None, scale, write, after, wait, ring, mixes, wide, True)

    @pl.loop(0, BLOCKS)
    def _(block):
        copy_out(out, o_hbm, out_sem, block).wait()


def final_kernel(
    mix_ref,
    p_hbm,
    back_hbm,
    halo_ref,
    edge_ref,
    diff_ref,
    base_ref,
    obs_ref,
    o_hbm,
    s_hbm,
    src,
    out,
    in_sem,
    out_sem,
    ring,
    mixes,
    wide,
    back,
    state,
    back_sem,
    state_sem,
):
    @pl.loop(0, BLOCKS)
    def _(block):
        copy_in(p_hbm, src, in_sem, block).start()
        copy_in(back_hbm, back, back_sem, block).start()

    def write(block, level, mix, lap):
        at = rows_at(block)
        out[block, level] = base_ref[0, level, at, :] - (mix + diff_ref[0, at, :] * lap)
        state[block, level] = obs_ref[0, level, at, :] - back[block, level]

    def wait(block):
        copy_in(p_hbm, src, in_sem, block).wait()
        copy_in(back_hbm, back, back_sem, block).wait()

    def after(block):
        copy_out(out, o_hbm, out_sem, block).start()
        @pl.when(block == 0)
        def _():
            for level in range(LEV):
                state[0, level, 0:1, :] = state[0, level, 0:1, :] - edge_ref[level]

        @pl.when(block == BLOCKS - 1)
        def _():
            for level in range(LEV):
                at = SUBL - 1
                state[BLOCKS - 1, level, at:, :] = state[BLOCKS - 1, level, at:, :] - edge_ref[LEV + level]

        copy_out(state, s_hbm, state_sem, block).start()

    lo_ref, hi_ref = halo_ref.at[pl.ds(0, LEV)], halo_ref.at[pl.ds(LEV, LEV)]
    stencil_steps(
        mix_ref, src, lo_ref, hi_ref, lambda field, block: field, write, after, wait, ring, mixes, wide, False
    )

    @pl.loop(0, BLOCKS)
    def _(block):
        copy_out(out, o_hbm, out_sem, block).wait()
        copy_out(state, s_hbm, state_sem, block).wait()


FIELD = jax.ShapeDtypeStruct((1, LEV, CX, NY), F32)
STENCIL_SCRATCH = [
    pltpu.VMEM((BLOCKS, LEV, SUBL, NY), F32),
    pltpu.VMEM((BLOCKS, LEV, SUBL, NY), F32),
    pltpu.SemaphoreType.DMA((BLOCKS,)),
    pltpu.SemaphoreType.DMA((BLOCKS,)),
    pltpu.VMEM((3, LEV, SUBL, NY), F32),
    pltpu.VMEM((2, WIDE, NY), F32),
    pltpu.VMEM((2, WIDE, WIDE), BF16),
]


def final_of(mix, prior, back, halo, edges, diff, base, with_obs):
    return pl.pallas_call(
        final_kernel,
        out_shape=[FIELD, FIELD],
        in_specs=[vmem_spec(), any_spec(), any_spec()] + [vmem_spec()] * 5,
        out_specs=[any_spec(), any_spec()],
        scratch_shapes=STENCIL_SCRATCH
        + [pltpu.VMEM((BLOCKS, LEV, SUBL, NY), F32)] * 2
        + [pltpu.SemaphoreType.DMA((BLOCKS,))] * 2,
        compiler_params=pltpu.CompilerParams(vmem_limit_bytes=30 << 20),
        cost_estimate=pl.CostEstimate(flops=2_000_000_000, bytes_accessed=24_000_000, transcendentals=0),
        name="final",
    )(mix, prior, back, halo, edges, diff, base, with_obs)


def adjoint_of(mix, dual, diff):
    return pl.pallas_call(
        adjoint_kernel,
        out_shape=FIELD,
        in_specs=[vmem_spec(), any_spec(), vmem_spec()],
        out_specs=any_spec(),
        scratch_shapes=STENCIL_SCRATCH,
        compiler_params=pltpu.CompilerParams(vmem_limit_bytes=VMEM_LIMIT),
        cost_estimate=pl.CostEstimate(flops=2_000_000_000, bytes_accessed=12_000_000, transcendentals=0),
        name="adjoint",
    )(mix, dual, diff)


def whole_spec(shape):
    return pl.BlockSpec(shape, lambda g: (0,) * len(shape))


BLOCK, DIFF = ((1, LEV, SUBL, NY), 2), ((1, SUBL, NY), 1)
EDGES = (2 * LEV, 1, NY)


def place(tile_ref, count, step):
    for tile in range(16):
        count[tile] = 0

    @pl.loop(0, NBLOCK)
    def _(j):
        tile = tile_ref[j]
        slot = count[tile]
        count[tile] = slot + 1
        step(j, tile * MOST + slot)


def prepare_kernel(
    tile_ref, d_ref, x0_ref, x7_ref, m0_ref, m7_ref, f0_ref, f7_ref, o_ref, first_ref, last_ref, count
):
    for level in range(LEV):
        first_ref[level] = x0_ref[0, level, 0:1, :]
        last_ref[level] = x7_ref[0, level, SUBL - 1 : SUBL, :]
        first_ref[LEV + level] = m0_ref[0, level, 0:1, :] * f0_ref[0, 0:1, :]
        last_ref[LEV + level] = m7_ref[0, level, SUBL - 1 : SUBL, :] * f7_ref[0, SUBL - 1 : SUBL, :]
    o_ref[...] = jnp.zeros((SLOTS, LEV, OB), F32)

    def step(j, at):
        o_ref[at] = d_ref[j]

    place(tile_ref, count, step)


def prepare(tile, blocks, x, dual, diff):
    def at(place, shape, dim):
        return pl.BlockSpec(shape, lambda g: tuple(place if d == dim else 0 for d in range(len(shape))))

    end = BLOCKS - 1
    return pl.pallas_call(
        prepare_kernel,
        out_shape=[jax.ShapeDtypeStruct((SLOTS, LEV, OB), F32)] + [jax.ShapeDtypeStruct(EDGES, F32)] * 2,
        grid=(1,),
        in_specs=[
            pl.BlockSpec(memory_space=pltpu.SMEM),
            whole_spec((NBLOCK, LEV, OB)),
            at(0, *BLOCK),
            at(end, *BLOCK),
            at(0, *BLOCK),
            at(end, *BLOCK),
            at(0, *DIFF),
            at(end, *DIFF),
        ],
        out_specs=[whole_spec((SLOTS, LEV, OB)), whole_spec(EDGES), whole_spec(EDGES)],
        scratch_shapes=[pltpu.SMEM((16,), jnp.int32)],
        compiler_params=pltpu.CompilerParams(vmem_limit_bytes=VMEM_LIMIT),
        cost_estimate=pl.CostEstimate(flops=1_000_000, bytes_accessed=4_000_000, transcendentals=0),
        name="prepare",
    )(tile, blocks, x, x, dual, dual, diff, diff)


def unpack_kernel(tile_ref, got_ref, var_ref, d_ref, o_ref, count):
    def step(j, at):
        o_ref[j] = var_ref[j] * d_ref[j] + got_ref[at]

    place(tile_ref, count, step)


def unpack(tile, got, var, blocks):
    return pl.pallas_call(
        unpack_kernel,
        out_shape=jax.ShapeDtypeStruct((NBLOCK, LEV, OB), F32),
        in_specs=[pl.BlockSpec(memory_space=pltpu.SMEM)] + [vmem_spec()] * 3,
        out_specs=vmem_spec(),
        scratch_shapes=[pltpu.SMEM((16,), jnp.int32)],
        compiler_params=pltpu.CompilerParams(vmem_limit_bytes=8 << 20),
        cost_estimate=pl.CostEstimate(flops=1_000_000, bytes_accessed=3_000_000, transcendentals=0),
        name="unpack",
    )(tile, got, var, blocks)


def moved(block, dtm, dspace):
    ntm, nspace = lax.axis_size("tm"), lax.axis_size("space")
    pairs = [
        (t * nspace + s, ((t + dtm) % ntm) * nspace + s + dspace)
        for t in range(ntm)
        for s in range(nspace)
        if 0 <= s + dspace < nspace
    ]
    return lax.ppermute(block, ("tm", "space"), pairs)


def on_device(
    dual_model,
    state_incr,
    dual_obs,
    model_var,
    obs_var,
    level_mix,
    diffusivity,
    obs_tile,
    obs_cells,
    obs_weights,
):
    tile = obs_tile.reshape(NBLOCK)
    packed, first, last = prepare(tile, dual_obs[0], state_incr, dual_model, diffusivity)
    lo, hi = moved(last, 0, 1), moved(first, 0, -1)
    got_dual = lax.all_to_all(packed, "space", split_axis=0, concat_axis=0, tiled=True)

    diff, packed = lax.optimization_barrier((diffusivity, packed))
    adjoint = adjoint_of(level_mix, dual_model, diff)
    sent, adjoint, got_dual, lo, hi, field = lax.optimization_barrier(
        (state_incr, adjoint, got_dual, lo, hi, state_incr)
    )
    prior = moved(sent, 1, 0)
    back = moved(adjoint, -1, 0)
    halo = moved(jnp.concatenate([lo[:LEV], hi[:LEV]]), 1, 0)
    edges = moved(jnp.concatenate([lo[LEV:], hi[LEV:]]), -1, 0)

    cells = obs_cells.reshape(SLOTS, TAPS, OB)
    weights = obs_weights.reshape(SLOTS, TAPS, OB)
    rows, quarter = cells & (TROWS - 1), lax.shift_right_logical(cells, 13)
    interp = gather(rows, field.reshape(LEV * CX, NY), quarter, weights)
    interp, got_dual = lax.optimization_barrier((interp, got_dual))
    got_interp = lax.all_to_all(interp, "space", split_axis=0, concat_axis=0, tiled=True)
    with_obs = scatter(rows, got_dual, dual_model.reshape(LEV * CX, NY), quarter, weights)

    with_obs, var = lax.optimization_barrier((with_obs, model_var))
    base = var * dual_model + state_incr
    base, with_obs = lax.optimization_barrier((base, with_obs))
    model_rows, state_rows = final_of(
        level_mix, prior, back, halo, edges, diffusivity, base, with_obs.reshape(1, LEV, CX, NY)
    )
    state_rows, var_obs = lax.optimization_barrier((state_rows, obs_var))
    obs_rows = unpack(tile, got_interp, var_obs[0], dual_obs[0])
    return (model_rows, obs_rows[None], state_rows)


def solution(mesh):
    field = P("tm", None, "space", None)
    blocks = P("tm", "space", None, None)
    taps = P("tm", "space", None, None, None, None)
    placed = (
        field,
        field,
        blocks,
        field,
        blocks,
        P("tm", None, None),
        P("tm", "space", None),
        P("tm", "space", None),
        taps,
        taps,
    )
    return jax.shard_map(
        on_device,
        mesh=mesh,
        in_specs=placed,
        out_specs=(field, blocks, field),
        check_vma=False,
    )
```
